512 devices in a mesh: leaf: 128 (over y, z, core), panel: 4 (over x).
Axes of the slice: x: 4, y: 8, z: 8, core: 2. Of those that a mesh axis runs over, the one named last changes fastest.
Arguments:
- leaf_rhs: bfloat16 [4, 128, 2, 128, 128], P('panel', 'leaf'), may hold values from -6 to 6
- leaf_inverse: bfloat16 [4, 128, 2, 128, 128], P('panel', 'leaf'), may hold values from -4 to 4, as said below
- leaf_panel: bfloat16 [4, 128, 2, 6, 128, 128], P('panel', 'leaf'), may hold values from -0.25 to 0.25
- panel_rows: int32 [4, 128, 2, 6], P('panel', 'leaf'), may hold values from 0 to 23, all different within a row
- live_count: int32 [4, 128], P('panel', 'leaf'), may hold values from 1 to 2, 192 in all within a row
- sep1_rhs: bfloat16 [4, 128, 128, 128], P('panel', 'leaf'), may hold values from -6 to 6
- sep1_inverse: bfloat16 [4, 128, 1024, 128], P('panel', 'leaf'), may hold values from -4 to 4, as said below
- sep1_panel: bfloat16 [4, 128, 2048, 128], P('panel', 'leaf'), may hold values from -0.125 to 0.125
- sep2_rhs: bfloat16 [4, 128, 128, 128], P('panel', 'leaf'), may hold values from -6 to 6
- sep2_inverse: bfloat16 [4, 128, 2048, 128], P('panel', 'leaf'), may hold values from -4 to 4, as said below
Outputs:
- leaf_sample: bfloat16 [4, 128, 2, 128, 128], P('panel', 'leaf')
- sep1_sample: bfloat16 [4, 128, 128, 128], P('panel', 'leaf')
- sep2_sample: bfloat16 [4, 128, 128, 128], P('panel', 'leaf')
The draws below stay inside these ranges and needn't reach their ends.
Inputs may be any that keep to these rules, and one draw needn't show every extreme that they name: `panel_rows`: the 6 row block indices of one slot differ. `live_count`: slots at or beyond the count hold no supernode. `leaf_inverse`: zero above the diagonal of each 128 by 128 block. `sep1_inverse`: zero above the diagonal of the assembled separator block. `sep2_inverse`: zero above the diagonal of the assembled separator block.
All inputs are finite; a program needn't handle non-finite values. No bound on the sum of `live_count` on one device may be relied on, other than what follows from the above.
Results may differ from the reference program's by a relative error of at most 0.024.
Values may be sent and summed in bfloat16 or wider, within the bound.
No kernel may reach another device: no remote copies, remote signals or barrier semaphores. Data moves between devices by JAX's collectives and lax.ppermute only.
A program may use at most 64 MiB of HBM per device.

```python
import math
import jax
import jax.numpy as jnp
import numpy as np
from jax import lax

W = 128
SAMPLES = 128
SLOTS = 2
NNZ = 6
PANELS = 4
LEAVES = 128
BLOCKS = 24
SEP1 = 1024
SEP2 = 2048


def triangle(key, rows_index, columns_index, order, array_shape):
    diagonal_key, lower_key = jax.random.split(key)
    diagonal = jax.random.uniform(diagonal_key, array_shape, jnp.float32, 0.6, 1.4)
    lower_part = jax.random.normal(lower_key, array_shape, jnp.float32) * (0.6 / order ** 0.5)
    lower_part = jnp.clip(lower_part, -3.0, 3.0)
    return jnp.where(rows_index == columns_index, diagonal, jnp.where(rows_index > columns_index, lower_part, 0.0))


def draw_leaf_inverse(key, part):
    key = jax.random.fold_in(key, 11)
    array_shape = (PANELS, LEAVES, SLOTS, W, W)
    rows_index = lax.broadcasted_iota(jnp.int32, array_shape, 3)
    columns_index = lax.broadcasted_iota(jnp.int32, array_shape, 4)
    return triangle(key, rows_index, columns_index, W, array_shape).astype(jnp.bfloat16)


def separator_inverse(key, group_size, height):
    array_shape = (PANELS, LEAVES, height, W)
    panel_index = lax.broadcasted_iota(jnp.int32, array_shape, 0)
    leaf_index = lax.broadcasted_iota(jnp.int32, array_shape, 1)
    rows_index = lax.broadcasted_iota(jnp.int32, array_shape, 2)
    columns_index = (leaf_index % group_size * PANELS + panel_index) * W + lax.broadcasted_iota(jnp.int32, array_shape, 3)
    return triangle(key, rows_index, columns_index, height, array_shape).astype(jnp.bfloat16)


def draw_sep1_inverse(key, part):
    key = jax.random.fold_in(key, 12)
    return separator_inverse(key, 2, SEP1)


def draw_sep2_inverse(key, part):
    key = jax.random.fold_in(key, 13)
    return separator_inverse(key, 4, SEP2)


def block_levels(rng, extent, cuts, smallest, largest):
    level = 1.0
    for axis_at, shards_of in cuts:
        heights = jax.random.uniform(jax.random.fold_in(jax.random.fold_in(rng, 6), axis_at), (shards_of,), jnp.float32, smallest / len(cuts), largest / len(cuts))
        level = level * jnp.repeat(jnp.exp(heights), extent[axis_at] // shards_of).reshape((-1,) + (1,) * (len(extent) - 1 - axis_at))
    return level


def distinct(rng, rows, count, top, lift):
    order = jax.random.permutation(jax.random.fold_in(rng, 1), count)
    pull = order
    for power in range(3):
        pull = pull * pull // count
    pull = pull * lift // count
    lots = jax.random.randint(jax.random.fold_in(rng, 2), (rows, count), 0, 4096) + pull
    holders = jax.random.permutation(jax.random.fold_in(rng, 3), rows)[jnp.arange(count) % rows]
    lots = jnp.where(jnp.arange(rows)[:, None] == holders[None, :], 1 << 14, lots)
    priority = lots * count + jnp.arange(count)
    return lax.top_k(priority.astype(jnp.int32), top)[1].astype(jnp.int32)


def profile(count, total, reach, slope):
    weights = [(1 << 20) // math.isqrt(standing ** slope) + 1 for standing in range(2, count + 1)]
    surplus, holding = total - reach - (count - 1), [1] * (count - 1)
    while surplus > 0:
        movable = [i for i in range(count - 1) if holding[i] < reach]
        mass, remaining = sum([weights[i] for i in movable]), surplus
        for i in movable:
            addition = min(reach - holding[i], max(1, remaining * weights[i] // mass), surplus)
            holding[i] = holding[i] + addition
            surplus = surplus - addition
    return np.array([reach] + holding)


def ragged_sizes(rng, number_of, total, most, slope):
    if number_of == 2:
        one = jax.random.randint(rng, (), max(1, total - most), min(most, total - 1) + 1)
        return jnp.stack([one, total - one])
    sizes = jnp.asarray(profile(number_of, total, most, slope), jnp.int32)
    twos = (number_of - 1) // 2
    source_of, receiver = sizes[1:1 + 2 * twos:2], sizes[2:2 + 2 * twos:2]
    margin = jnp.minimum(source_of - 1, most - receiver)
    moved = jax.random.randint(jax.random.fold_in(rng, 1), (twos,), 0, 1 << 20) % (margin + 1)
    sizes = sizes.at[1:1 + 2 * twos:2].set(source_of - moved).at[2:2 + 2 * twos:2].set(receiver + moved)
    return sizes[jax.random.permutation(jax.random.fold_in(rng, 2), number_of)]


def normal_values(stream_key, shape, spread, most, shards=(), dtype=jnp.bfloat16):
    loudness = block_levels(stream_key, shape, shards, -0.22, 0.18) if shards else 1.0
    drawn = jax.random.normal(stream_key, shape, jnp.float32) * spread * loudness
    return jnp.minimum(jnp.maximum(drawn, -most), most).astype(dtype)


def setup_inputs(seed: int = 0) -> dict:
    key_of = jax.random.split(jax.random.key(seed), 11)
    leaf_rhs = normal_values(key_of[0], (PANELS, LEAVES, SLOTS, W, SAMPLES), 1.0, 6.0, ((0, 4), (1, 128)))
    leaf_inverse = draw_leaf_inverse(jax.random.fold_in(key_of[10], 71), 0)
    leaf_panel = normal_values(key_of[2], (PANELS, LEAVES, SLOTS, NNZ, W, W), (W * SLOTS * NNZ // 3) ** -0.5, 0.25, ((0, 4), (1, 128)))
    panel_rows = distinct(key_of[3], PANELS * LEAVES * SLOTS, BLOCKS, NNZ, 2048).reshape((PANELS, LEAVES, SLOTS, NNZ))
    live_count = jax.vmap(lambda own: ragged_sizes(own, LEAVES, LEAVES * (SLOTS + 1) // 2, SLOTS, 2))(jax.random.split(key_of[4], PANELS)).reshape((PANELS, LEAVES)).astype(jnp.int32)
    sep1_rhs = normal_values(key_of[5], (PANELS, LEAVES, W, SAMPLES), 1.0, 6.0, ((0, 4), (1, 128)))
    sep1_inverse = draw_sep1_inverse(jax.random.fold_in(key_of[10], 71), 0)
    sep1_panel = normal_values(key_of[7], (PANELS, LEAVES, SEP2, W), (2 * SEP1) ** -0.5, 0.125, ((0, 4), (1, 128)))
    sep2_rhs = normal_values(key_of[8], (PANELS, LEAVES, W, SAMPLES), 1.0, 6.0, ((0, 4), (1, 128)))
    sep2_inverse = draw_sep2_inverse(jax.random.fold_in(key_of[10], 71), 0)
    return dict(leaf_rhs=leaf_rhs, leaf_inverse=leaf_inverse, leaf_panel=leaf_panel, panel_rows=panel_rows, live_count=live_count, sep1_rhs=sep1_rhs, sep1_inverse=sep1_inverse, sep1_panel=sep1_panel, sep2_rhs=sep2_rhs, sep2_inverse=sep2_inverse)


def pieces_matrix(columns, group_size):
    lead, leaves, height, block_width = columns.shape
    shaped = columns.reshape(lead, leaves // group_size, group_size, height, block_width)
    return jnp.transpose(shaped, (1, 3, 2, 0, 4)).reshape(leaves // group_size, height, group_size * lead * block_width)


def pieces_vector(pieces, group_size):
    lead, leaves, block_width, samples = pieces.shape
    shaped = pieces.reshape(lead, leaves // group_size, group_size, block_width, samples)
    return jnp.transpose(shaped, (1, 2, 0, 3, 4)).reshape(leaves // group_size, group_size * lead * block_width, samples)


def vector_pieces(vectors, group_size):
    groups, height, samples = vectors.shape
    shaped = vectors.reshape(groups, group_size, PANELS, W, samples)
    return jnp.transpose(shaped, (2, 0, 1, 3, 4)).reshape(PANELS, groups * group_size, W, samples)


def device_terms(columns, pieces, group_size):
    def leaf_terms_one(inputs):
        column_leaf, piece_leaf = inputs
        summed_all = jnp.zeros((column_leaf.shape[1], piece_leaf.shape[-1]), jnp.float32)
        for panel_place in range(PANELS):
            product = jnp.dot(column_leaf[panel_place], piece_leaf[panel_place], preferred_element_type=jnp.float32)
            summed_all = summed_all + lax.optimization_barrier(product.astype(jnp.bfloat16)).astype(jnp.float32)
        return summed_all
    per_leaf = lax.map(leaf_terms_one, (jnp.swapaxes(columns, 0, 1), jnp.swapaxes(pieces, 0, 1)))
    leaves = per_leaf.shape[0]
    return per_leaf.reshape((leaves // group_size, group_size) + per_leaf.shape[1:]).sum(axis=1)


def leaf_forward(inverse, right_side, panels, row_blocks, live_total):
    live_mask = (jnp.arange(SLOTS) < live_total).astype(jnp.float32)
    solved = jnp.einsum('sab,sbn->san', inverse.astype(jnp.float32), right_side.astype(jnp.float32))
    solved = (solved * live_mask[:, None, None]).astype(jnp.bfloat16)
    products = jnp.einsum('skab,sbn->skan', panels.astype(jnp.float32), solved.astype(jnp.float32))
    selector = (row_blocks[..., None] == jnp.arange(BLOCKS)).astype(jnp.float32)
    leaf_terms = jnp.einsum('skq,skan->qan', selector, products)
    return solved, leaf_terms


def leaf_backward(inverse, panels, row_blocks, live_total, solved, ancestors):
    live_mask = (jnp.arange(SLOTS) < live_total).astype(jnp.float32)
    picked = ancestors[row_blocks]
    correction = jnp.einsum('skab,skan->sbn', panels.astype(jnp.float32), picked.astype(jnp.float32))
    shifted = (solved.astype(jnp.float32) - correction).astype(jnp.bfloat16)
    result = jnp.einsum('sab,san->sbn', inverse.astype(jnp.float32), shifted.astype(jnp.float32))
    return (result * live_mask[:, None, None]).astype(jnp.bfloat16)


def reference(leaf_rhs, leaf_inverse, leaf_panel, panel_rows, live_count, sep1_rhs, sep1_inverse, sep1_panel, sep2_rhs, sep2_inverse):
    def leaf_step(inputs):
        inverse_leaf, right_leaf, panel_leaf, rows_leaf, count_leaf = inputs
        solved_list = []
        summed_all = jnp.zeros((BLOCKS, W, SAMPLES), jnp.float32)
        for panel_place in range(PANELS):
            solved, leaf_terms = leaf_forward(inverse_leaf[panel_place], right_leaf[panel_place], panel_leaf[panel_place], rows_leaf[panel_place], count_leaf[panel_place])
            solved_list.append(solved)
            summed_all = summed_all + lax.optimization_barrier(leaf_terms.astype(jnp.bfloat16)).astype(jnp.float32)
        return jnp.stack(solved_list), summed_all

    swapped = tuple(jnp.swapaxes(array_in, 0, 1) for array_in in (leaf_inverse, leaf_rhs, leaf_panel, panel_rows, live_count))
    leaf_solved, leaf_sums = lax.map(leaf_step, swapped)
    first_count = 2 * PANELS
    first_terms = leaf_sums[:, :first_count].reshape(LEAVES // 2, 2, first_count, W, SAMPLES).sum(axis=1).reshape(LEAVES // 2, SEP1, SAMPLES)
    second_terms = leaf_sums[:, first_count:].reshape(LEAVES // 4, 4, BLOCKS - first_count, W, SAMPLES).sum(axis=1).reshape(LEAVES // 4, SEP2, SAMPLES)
    first_side = (pieces_vector(sep1_rhs, 2).astype(jnp.float32) - first_terms).astype(jnp.bfloat16)
    solved1 = device_terms(sep1_inverse, vector_pieces(first_side, 2), 2).astype(jnp.bfloat16)
    raised = device_terms(sep1_panel, vector_pieces(solved1, 2), 4)
    second_side = (pieces_vector(sep2_rhs, 4).astype(jnp.float32) - (second_terms + raised)).astype(jnp.bfloat16)
    solved2 = device_terms(sep2_inverse, vector_pieces(second_side, 4), 4).astype(jnp.bfloat16)
    inverse_second = pieces_matrix(sep2_inverse, 4).astype(jnp.float32)
    sample2 = jnp.einsum('jab,jan->jbn', inverse_second, solved2.astype(jnp.float32)).astype(jnp.bfloat16)
    panel_first = pieces_matrix(sep1_panel, 2).astype(jnp.float32)
    above_values = jnp.repeat(sample2, 2, axis=0).astype(jnp.float32)
    correction = jnp.einsum('jab,jan->jbn', panel_first, above_values)
    shifted1 = (solved1.astype(jnp.float32) - correction).astype(jnp.bfloat16)
    inverse_first = pieces_matrix(sep1_inverse, 2).astype(jnp.float32)
    sample1 = jnp.einsum('jab,jan->jbn', inverse_first, shifted1.astype(jnp.float32)).astype(jnp.bfloat16)
    ancestors = jnp.concatenate([jnp.repeat(sample1, 2, axis=0), jnp.repeat(sample2, 4, axis=0)], axis=1)
    ancestors = ancestors.reshape(LEAVES, BLOCKS, W, SAMPLES)

    def leaf_back_step(inputs):
        inverse_leaf, panel_leaf, rows_leaf, count_leaf, solved_leaf, ancestor_leaf = inputs
        outputs = []
        for panel_place in range(PANELS):
            outputs.append(leaf_backward(inverse_leaf[panel_place], panel_leaf[panel_place], rows_leaf[panel_place], count_leaf[panel_place], solved_leaf[panel_place], ancestor_leaf))
        return jnp.stack(outputs)

    back_inputs = (jnp.swapaxes(leaf_inverse, 0, 1), jnp.swapaxes(leaf_panel, 0, 1), jnp.swapaxes(panel_rows, 0, 1), jnp.swapaxes(live_count, 0, 1), leaf_solved, ancestors)
    leaf_sample = lax.map(leaf_back_step, back_inputs)
    return jnp.swapaxes(leaf_sample, 0, 1), vector_pieces(sample1, 2), vector_pieces(sample2, 4)
```

```python
import jax
import jax.numpy as jnp
from jax import lax
from jax.sharding import Mesh, PartitionSpec as P

FIRST = ("core", "panel")
SECOND = ("pair", "core", "panel")


def owned_sum(partials, axes):
    received = lax.all_to_all(partials, axes, 0, 0, tiled=True)
    return received.astype(jnp.float32).sum(axis=0)


def spread(piece, axes):
    size = 1
    for name in axes:
        size = size * lax.axis_size(name)
    copies = jnp.broadcast_to(piece[None], (size,) + piece.shape)
    return lax.all_to_all(copies, axes, 0, 0, tiled=True)


def gather(piece, axes):
    return lax.all_gather(piece[None], axes, axis=0, tiled=True)


def apply_columns(columns, piece, width):
    product = jnp.dot(columns, piece, preferred_element_type=jnp.float32)
    return product.reshape(-1, width, piece.shape[-1])


def contract_rows(matrix, vectors):
    vectors = vectors.reshape(-1, vectors.shape[-1])
    return lax.dot_general(
        matrix, vectors, (((0,), (0,)), ((), ())), preferred_element_type=jnp.float32
    )


def body(
    leaf_rhs,
    leaf_inverse,
    leaf_panel,
    panel_rows,
    live_count,
    sep1_rhs,
    sep1_inverse,
    sep1_panel,
    sep2_rhs,
    sep2_inverse,
):
    right_side = leaf_rhs[0, 0]
    inverse = leaf_inverse[0, 0]
    panels = leaf_panel[0, 0]
    row_blocks = panel_rows[0, 0]
    slots, width = inverse.shape[0], inverse.shape[1]
    samples = right_side.shape[-1]
    first_blocks = sep1_inverse.shape[2] // width
    second_blocks = sep2_inverse.shape[2] // width
    live = (jnp.arange(slots, dtype=jnp.int32) < live_count[0, 0]).astype(jnp.float32)

    leaf_solved = jnp.einsum(
        "sab,sbn->san", inverse, right_side, preferred_element_type=jnp.float32
    )
    leaf_solved = (leaf_solved * live[:, None, None]).astype(jnp.bfloat16)
    products = jnp.einsum("skab,sbn->skan", panels, leaf_solved, preferred_element_type=jnp.float32)
    leaf_terms = (
        jnp.zeros((first_blocks + second_blocks, width, samples), jnp.float32)
        .at[row_blocks.reshape(-1)]
        .add(products.reshape(-1, width, samples))
    )

    own_first = owned_sum(leaf_terms[:first_blocks].astype(jnp.bfloat16), FIRST)
    first_side = (sep1_rhs[0, 0].astype(jnp.float32) - own_first).astype(jnp.bfloat16)
    partial1 = apply_columns(sep1_inverse[0, 0], first_side, width)
    solved1 = owned_sum(partial1.astype(jnp.bfloat16), FIRST).astype(jnp.bfloat16)

    raised = apply_columns(sep1_panel[0, 0], solved1, width)
    own_second = owned_sum((leaf_terms[first_blocks:] + raised).astype(jnp.bfloat16), SECOND)
    second_side = (sep2_rhs[0, 0].astype(jnp.float32) - own_second).astype(jnp.bfloat16)
    partial2 = apply_columns(sep2_inverse[0, 0], second_side, width)
    solved2 = owned_sum(partial2.astype(jnp.bfloat16), SECOND).astype(jnp.bfloat16)

    whole_solved = gather(solved2, SECOND)
    sample2 = contract_rows(sep2_inverse[0, 0], whole_solved).astype(jnp.bfloat16)
    whole_second = spread(sample2, SECOND)
    correction = contract_rows(sep1_panel[0, 0], whole_second)
    shifted1 = (solved1.astype(jnp.float32) - correction).astype(jnp.bfloat16)
    whole_shifted = gather(shifted1, FIRST)
    sample1 = contract_rows(sep1_inverse[0, 0], whole_shifted).astype(jnp.bfloat16)
    whole_first = spread(sample1, FIRST)

    ancestors = jnp.concatenate([whole_first, whole_second], 0)
    picked = ancestors[row_blocks]
    correction_all = jnp.einsum("skab,skan->sbn", panels, picked, preferred_element_type=jnp.float32)
    leaf_shifted = (leaf_solved.astype(jnp.float32) - correction_all).astype(jnp.bfloat16)
    leaf_sample = jnp.einsum(
        "sab,san->sbn", inverse, leaf_shifted, preferred_element_type=jnp.float32
    )
    leaf_sample = (leaf_sample * live[:, None, None]).astype(jnp.bfloat16)
    return (leaf_sample[None, None], sample1[None, None], sample2[None, None])


def solution(mesh):
    places = mesh.devices.reshape(-1, 2, 2, mesh.shape["panel"])
    fine = Mesh(places, ("group", "pair", "core", "panel"))
    leaf = ("group", "pair", "core")

    def spec(rank):
        return P("panel", leaf, *(None,) * (rank - 2))

    return jax.shard_map(
        body,
        mesh=fine,
        in_specs=tuple(spec(rank) for rank in (5, 5, 6, 4, 2, 4, 4, 4, 4, 4)),
        out_specs=tuple(spec(rank) for rank in (5, 4, 4)),
        check_vma=False,
    )
```

```python
import jax
import jax.numpy as jnp
from jax import lax
from jax.experimental import pallas as pl
from jax.experimental.pallas import tpu as pltpu
from jax.sharding import Mesh, PartitionSpec as P

FIRST = ("core", "panel")
SECOND = ("pair", "core", "panel")
CHIPS = ("pair", "panel")


def block_dot(left, right):
    return lax.dot_general(
        left, right, (((left.ndim - 1,), (0,)), ((), ())), preferred_element_type=jnp.float32
    )


def leaf_forward_kernel(rows, count, rhs, inverse, panels, solved, first, second, total):
    slots, touched, width, samples = panels.shape[0], panels.shape[1], rhs.shape[1], rhs.shape[2]
    total[...] = jnp.zeros_like(total)
    for s in range(slots):
        live = jnp.where(s < count[0, 0], 1.0, 0.0)
        piece = (block_dot(inverse[s], rhs[s]) * live).astype(jnp.bfloat16)
        solved[s] = piece
        products = block_dot(panels[s].reshape(touched * width, width), piece)
        products = products.reshape(touched, width, samples)
        for k in range(touched):
            total[rows[s, k]] += products[k]
    split = first.shape[0]
    first[...] = total[:split].astype(jnp.bfloat16)
    second[...] = total[split:]


def leaf_forward(rows, count, rhs, inverse, panels, first_blocks, second_blocks):
    width, samples = rhs.shape[1:]
    smem = pl.BlockSpec(memory_space=pltpu.SMEM)
    vmem = pl.BlockSpec(memory_space=pltpu.VMEM)
    return pl.pallas_call(
        leaf_forward_kernel,
        out_shape=(
            jax.ShapeDtypeStruct(rhs.shape, jnp.bfloat16),
            jax.ShapeDtypeStruct((first_blocks, width, samples), jnp.bfloat16),
            jax.ShapeDtypeStruct((second_blocks, width, samples), jnp.float32),
        ),
        in_specs=[smem, smem, vmem, vmem, vmem],
        out_specs=(vmem, vmem, vmem),
        scratch_shapes=[pltpu.VMEM((first_blocks + second_blocks, width, samples), jnp.float32)],
        compiler_params=pltpu.CompilerParams(vmem_limit_bytes=16 << 20),
        name="leaf_forward",
    )(rows, count, rhs, inverse, panels)


def side_kernel(received, rhs, columns, partials):
    side = rhs[...].astype(jnp.float32) - received[...].astype(jnp.float32).sum(axis=0)
    product = block_dot(columns[...], side.astype(jnp.bfloat16))
    partials[...] = product.reshape(partials.shape).astype(jnp.bfloat16)


def side_partials(received, rhs, columns):
    vmem = pl.BlockSpec(memory_space=pltpu.VMEM)
    return pl.pallas_call(
        side_kernel,
        out_shape=jax.ShapeDtypeStruct(received.shape, jnp.bfloat16),
        in_specs=[vmem] * 3,
        out_specs=vmem,
        compiler_params=pltpu.CompilerParams(vmem_limit_bytes=16 << 20),
        name="side_partials",
    )(received, rhs, columns)


def raise_kernel(received, terms, columns, solved, raised):
    piece = received[...].astype(jnp.float32).sum(axis=0).astype(jnp.bfloat16)
    solved[...] = piece
    product = block_dot(columns[...], piece).reshape(raised.shape)
    raised[...] = (product + terms[...]).astype(jnp.bfloat16)


def raise_terms(received, terms, columns):
    vmem = pl.BlockSpec(memory_space=pltpu.VMEM)
    return pl.pallas_call(
        raise_kernel,
        out_shape=(
            jax.ShapeDtypeStruct(received.shape[1:], jnp.bfloat16),
            jax.ShapeDtypeStruct(terms.shape, jnp.bfloat16),
        ),
        in_specs=[vmem] * 3,
        out_specs=(vmem, vmem),
        compiler_params=pltpu.CompilerParams(vmem_limit_bytes=16 << 20),
        name="raise_terms",
    )(received, terms, columns)


def leaf_backward_kernel(rows, count, first, second, panels, inverse, solved, sample, above):
    slots, touched, width = panels.shape[0], panels.shape[1], panels.shape[2]
    split = first.shape[0]
    above[:split] = first[...]
    above[split:] = second[...]
    contract = (((0,), (0,)), ((), ()))
    for s in range(slots):
        picked = jnp.concatenate([above[rows[s, k]] for k in range(touched)], axis=0)
        correction = lax.dot_general(
            panels[s].reshape(touched * width, width),
            picked,
            contract,
            preferred_element_type=jnp.float32,
        )
        shifted = (solved[s].astype(jnp.float32) - correction).astype(jnp.bfloat16)
        result = lax.dot_general(inverse[s], shifted, contract, preferred_element_type=jnp.float32)
        live = jnp.where(s < count[0, 0], 1.0, 0.0)
        sample[s] = (result * live).astype(jnp.bfloat16)


def leaf_backward(rows, count, first, second, panels, inverse, solved):
    smem = pl.BlockSpec(memory_space=pltpu.SMEM)
    vmem = pl.BlockSpec(memory_space=pltpu.VMEM)
    blocks = first.shape[0] + second.shape[0]
    return pl.pallas_call(
        leaf_backward_kernel,
        out_shape=jax.ShapeDtypeStruct(solved.shape, jnp.bfloat16),
        in_specs=[smem, smem] + [vmem] * 5,
        out_specs=vmem,
        scratch_shapes=[pltpu.VMEM((blocks,) + first.shape[1:], jnp.bfloat16)],
        compiler_params=pltpu.CompilerParams(vmem_limit_bytes=16 << 20),
        name="leaf_backward",
    )(rows, count, first, second, panels, inverse, solved)


def exchange(blocks, axes):
    return lax.all_to_all(blocks, axes, 0, 0, tiled=True)


def by_core(blocks, axis):
    other = lax.ppermute(blocks, "core", [(0, 1), (1, 0)])
    upper = lax.axis_index("core") == 1
    lower_part = jnp.where(upper, other, blocks)
    upper_part = jnp.where(upper, blocks, other)
    return jnp.stack([lower_part, upper_part], axis)


def copies(blocks, axes):
    size = 1
    for name in axes:
        size = size * lax.axis_size(name)
    return jnp.broadcast_to(blocks[None], (size,) + blocks.shape)


def spread_pairs(piece, axes):
    both = by_core(piece, 0)
    received = exchange(copies(both, axes), axes)
    panels = lax.axis_size("panel")
    received = received.reshape((-1, panels) + both.shape)
    return jnp.swapaxes(received, 1, 2).reshape((-1,) + piece.shape)


def spread_then_pair(piece, axes):
    received = exchange(copies(piece, axes), axes)
    panels = lax.axis_size("panel")
    received = received.reshape((-1, panels) + piece.shape)
    return by_core(received, 1).reshape((-1,) + piece.shape)


def contract_rows(matrix, vectors):
    vectors = vectors.reshape(-1, vectors.shape[-1])
    return lax.dot_general(
        matrix, vectors, (((0,), (0,)), ((), ())), preferred_element_type=jnp.float32
    )


def body(
    leaf_rhs,
    leaf_inverse,
    leaf_panel,
    panel_rows,
    live_count,
    sep1_rhs,
    sep1_inverse,
    sep1_panel,
    sep2_rhs,
    sep2_inverse,
):
    inverse, panels, row_blocks = leaf_inverse[0, 0], leaf_panel[0, 0], panel_rows[0, 0]
    width = inverse.shape[1]
    first_blocks = sep1_inverse.shape[2] // width
    second_blocks = sep2_inverse.shape[2] // width
    columns1, columns2, raising = sep1_inverse[0, 0], sep2_inverse[0, 0], sep1_panel[0, 0]

    leaf_solved, first_terms, second_terms = leaf_forward(
        row_blocks, live_count, leaf_rhs[0, 0], inverse, panels, first_blocks, second_blocks
    )
    partial1 = side_partials(exchange(first_terms, FIRST), sep1_rhs[0, 0], columns1)
    solved1, raised = raise_terms(exchange(partial1, FIRST), second_terms, raising)
    partial2 = side_partials(exchange(raised, SECOND), sep2_rhs[0, 0], columns2)
    received = exchange(partial2, SECOND)
    solved2 = received.astype(jnp.float32).sum(axis=0).astype(jnp.bfloat16)

    whole_solved = spread_pairs(solved2, CHIPS)
    sample2 = contract_rows(columns2, whole_solved).astype(jnp.bfloat16)
    whole_second = spread_then_pair(sample2, CHIPS)
    correction = contract_rows(raising, whole_second)
    shifted1 = (solved1.astype(jnp.float32) - correction).astype(jnp.bfloat16)
    whole_shifted = spread_pairs(shifted1, ("panel",))
    sample1 = contract_rows(columns1, whole_shifted).astype(jnp.bfloat16)
    whole_first = spread_then_pair(sample1, ("panel",))

    leaf_sample = leaf_backward(
        row_blocks, live_count, whole_first, whole_second, panels, inverse, leaf_solved
    )
    return (leaf_sample[None, None], sample1[None, None], sample2[None, None])


def solution(mesh):
    places = mesh.devices.reshape(-1, 2, 2, mesh.shape["panel"])
    fine = Mesh(places, ("group", "pair", "core", "panel"))
    leaf = ("group", "pair", "core")

    def spec(rank):
        return P("panel", leaf, *(None,) * (rank - 2))

    return jax.shard_map(
        body,
        mesh=fine,
        in_specs=tuple(spec(rank) for rank in (5, 5, 6, 4, 2, 4, 4, 4, 4, 4)),
        out_specs=tuple(spec(rank) for rank in (5, 4, 4)),
        check_vma=False,
    )
```

```python
import jax
import jax.numpy as jnp
from jax import lax
from jax.experimental import pallas as pl
from jax.experimental.pallas import tpu as pltpu
from jax.sharding import Mesh, PartitionSpec as P

FIRST = ("core", "panel")
CHIPS = ("pair", "panel")
LINE = ("panel",)
F32, BF16 = jnp.float32, jnp.bfloat16
VMEM = pl.BlockSpec(memory_space=pltpu.VMEM)
SMEM = pl.BlockSpec(memory_space=pltpu.SMEM)
HBM = pl.BlockSpec(memory_space=pltpu.HBM)
PARAMS = pltpu.CompilerParams(vmem_limit_bytes=24 << 20)


def in_hbm(*arrays):
    return [pltpu.with_memory_space_constraint(array, pltpu.HBM) for array in arrays]


def dot(left, right):
    return lax.dot_general(left, right, (((1,), (0,)), ((), ())), preferred_element_type=F32)


def half_lanes(block):
    return lax.broadcasted_iota(jnp.int32, block.shape, 1) < block.shape[1] // 2


def turned(block):
    return pltpu.roll(block, block.shape[1] // 2, 1)


def packed(lower, upper):
    low = half_lanes(lower)
    return jnp.where(low, lower, turned(upper)), jnp.where(low, turned(lower), upper)


def start_loads(sems, *pairs):
    loads = [pltpu.make_async_copy(*pair, sems.at[i]) for i, pair in enumerate(pairs)]
    for load in loads:
        load.start()
    return loads


def leaf_forward_kernel(
    rows_h, count, rhs, inverse, panels, side1, solved, send, above, total, *scratch
):
    rows, rhs_v, inverse_v, panels_v, side1_v, sems = scratch
    loads = start_loads(
        sems,
        (inverse, inverse_v),
        (rhs, rhs_v),
        (panels, panels_v),
        (side1, side1_v),
        (rows_h, rows),
    )
    slots, touched, width = panels_v.shape[:3]
    first_blocks = send.shape[0]
    half = first_blocks // 2
    total[...] = jnp.zeros_like(total)
    loads[0].wait()
    loads[1].wait()
    for s in range(slots):
        live = jnp.where(s < count[0, 0], 1.0, 0.0)
        solved[s] = (dot(inverse_v[s], rhs_v[s]) * live).astype(BF16)
    loads[2].wait()
    loads[4].wait()
    for s in range(slots):
        products = dot(panels_v[s].reshape(touched * width, width), solved[s])
        for k in range(touched):
            total[rows[s, k]] += products[k * width : (k + 1) * width]
    loads[3].wait()
    own = lax.axis_index("core") * half + lax.axis_index("panel")
    total[own] -= side1_v[...].astype(F32)
    for p in range(half):
        zero, one = packed(total[p], total[half + p])
        send[p] = zero.astype(BF16)
        send[half + p] = one.astype(BF16)
    above[...] = total[first_blocks:]


def leaf_forward(rows, count, rhs, inverse, panels, side1, first_blocks, second_blocks):
    block = rhs.shape[1:]
    return pl.pallas_call(
        leaf_forward_kernel,
        out_shape=(
            jax.ShapeDtypeStruct(rhs.shape, BF16),
            jax.ShapeDtypeStruct((first_blocks,) + block, BF16),
            jax.ShapeDtypeStruct((second_blocks,) + block, F32),
        ),
        in_specs=[HBM, SMEM] + [HBM] * 4,
        out_specs=(VMEM,) * 3,
        scratch_shapes=[
            pltpu.VMEM((first_blocks + second_blocks,) + block, F32),
            pltpu.SMEM(rows.shape, rows.dtype),
            pltpu.VMEM(rhs.shape, BF16),
            pltpu.VMEM(inverse.shape, BF16),
            pltpu.VMEM(panels.shape, BF16),
            pltpu.VMEM(side1.shape, BF16),
            pltpu.SemaphoreType.DMA((5,)),
        ],
        compiler_params=PARAMS,
        name="leaf_forward",
    )(*in_hbm(rows), count, *in_hbm(rhs, inverse, panels, side1))


def leaf_second_kernel(
    above, solved, side2, inverse1, panel1, inverse2, panels, inverse, *outputs_and_scratch
):
    store, keep, solved_t, panels_v, inverse_v, side2_v, sems = outputs_and_scratch
    rows1, rows2 = inverse1.shape[0], inverse2.shape[0]
    loads = start_loads(
        sems,
        (inverse1, store.at[0:rows1]),
        (panel1, store.at[rows1 : rows1 + rows2]),
        (inverse2, store.at[rows1 + rows2 : rows1 + 2 * rows2]),
        (panels, panels_v),
        (inverse, inverse_v),
        (side2, side2_v),
    )
    send = rows1 + 2 * rows2
    width = above.shape[1]
    line = above.shape[0] // 4
    core = lax.axis_index("core")
    own = (lax.axis_index("pair") * 2 + core) * line + lax.axis_index("panel")
    loads[5].wait()
    side = side2_v[...].astype(F32)
    for z in range(2):
        for p in range(line):
            at = z * 2 * line + p
            lower = above[at] - jnp.where(own == at, 1.0, 0.0) * side
            upper = above[at + line] - jnp.where(own == at + line, 1.0, 0.0) * side
            zero, one = packed(lower, upper)
            at = z * line + p
            keep[at] = jnp.where(core == 0, zero, one)
            away = jnp.where(core == 0, one, zero)
            store[send + at * width : send + (at + 1) * width] = away.astype(BF16)
    for s in range(solved.shape[0]):
        solved_t[s] = solved[s].astype(F32).T.astype(BF16)
    for load in loads[:5]:
        load.wait()


def leaf_second(above, solved, side2, inverse1, panel1, inverse2, panels, inverse):
    halves = above.shape[0] // 2
    rows = inverse1.shape[0] + panel1.shape[0] + inverse2.shape[0] + halves * above.shape[1]
    return pl.pallas_call(
        leaf_second_kernel,
        out_shape=(
            jax.ShapeDtypeStruct((rows, inverse1.shape[1]), BF16),
            jax.ShapeDtypeStruct((halves,) + above.shape[1:], F32),
            jax.ShapeDtypeStruct(solved.shape, BF16),
            jax.ShapeDtypeStruct(panels.shape, BF16),
            jax.ShapeDtypeStruct(inverse.shape, BF16),
        ),
        in_specs=[VMEM] * 2 + [HBM] * 6,
        out_specs=(VMEM,) * 5,
        scratch_shapes=[pltpu.VMEM(side2.shape, BF16), pltpu.SemaphoreType.DMA((6,))],
        compiler_params=PARAMS,
        name="leaf_second",
    )(above, solved, *in_hbm(side2, inverse1, panel1, inverse2, panels, inverse))


def column_products(piece, mine, other, first_row, row_count):
    low = half_lanes(piece)
    across = turned(piece)
    zero = jnp.zeros_like(piece)
    lower = (jnp.where(low, piece, zero), jnp.where(low, across, zero))
    upper = (jnp.where(low, zero, across), jnp.where(low, zero, piece))
    swap = lax.axis_index("core") == 1

    def ordered(two):
        return [jnp.where(swap, two[1], two[0]), jnp.where(swap, two[0], two[1])]

    weights = jnp.concatenate(ordered(lower) + ordered(upper), 0).astype(BF16)
    half = mine.shape[1] * 4
    parts = []
    for start in range(first_row, first_row + row_count, 2 * half):
        middle = start + half
        wide = jnp.concatenate(
            [
                mine[start:middle],
                other[start:middle],
                mine[middle : middle + half],
                other[middle : middle + half],
            ],
            1,
        )
        parts.append(dot(wide, weights))
    return parts


def side_partials(received, mine, other, first_row, row_count):
    width = mine.shape[1]

    def kernel(received, mine, other, partials):
        side = -received[...].astype(F32).sum(axis=0)
        side = side.astype(BF16).astype(F32)
        for z, part in enumerate(column_products(side, mine, other, first_row, row_count)):
            for p in range(4):
                partials[z * 4 + p] = part[p * width : (p + 1) * width].astype(BF16)

    return pl.pallas_call(
        kernel,
        out_shape=jax.ShapeDtypeStruct((row_count // width // 2,) + received.shape[1:], BF16),
        in_specs=[VMEM] * 3,
        out_specs=VMEM,
        compiler_params=PARAMS,
        name="side_partials",
    )(received, mine, other)


def raise_terms(received, keep, mine, other, first_row, row_count, terms_row):
    width = mine.shape[1]

    def kernel(received, keep, mine, other, raised, solved_t):
        piece = received[...].astype(F32).sum(axis=0)
        piece = piece.astype(BF16).astype(F32)
        for z, part in enumerate(column_products(piece, mine, other, first_row, row_count)):
            for p in range(4):
                at = z * 4 + p
                came = other[terms_row + at * width : terms_row + (at + 1) * width]
                terms = keep[at] + came.astype(F32)
                raised[at] = (part[p * width : (p + 1) * width] + terms).astype(BF16)
        solved_t[...] = piece.T.astype(BF16)

    return pl.pallas_call(
        kernel,
        out_shape=(
            jax.ShapeDtypeStruct(keep.shape, BF16),
            jax.ShapeDtypeStruct(received.shape[1:], BF16),
        ),
        in_specs=[VMEM] * 4,
        out_specs=(VMEM,) * 2,
        compiler_params=PARAMS,
        name="raise_terms",
    )(received, keep, mine, other)


def turn_kernel(received, copies):
    piece = received[...].astype(F32).sum(axis=0).T.astype(BF16)
    for i in range(copies.shape[0]):
        copies[i] = piece


def turned_sum(received):
    return pl.pallas_call(
        turn_kernel,
        out_shape=jax.ShapeDtypeStruct(received.shape, BF16),
        in_specs=[VMEM],
        out_specs=VMEM,
        compiler_params=PARAMS,
        name="turned_sum",
    )(received)


def back_step(whole, mine, other, first_row, targets, base=None):
    panels = 4
    half = whole.shape[1] // 2
    rows = pl.ds(first_row, 2 * whole.shape[0] * mine.shape[1])

    def kernel(whole, mine, other, *rest):
        pieces = []
        for z in range(whole.shape[0] // panels):
            for c in range(2):
                for p in range(panels):
                    pieces.append(whole[z * panels + p, c * half : (c + 1) * half])
        vectors = jnp.concatenate(pieces, 1)
        mine_t = dot(vectors, mine[rows])
        other_t = dot(vectors, other[rows])
        swap = lax.axis_index("core") == 1
        result = jnp.concatenate(
            [jnp.where(swap, other_t, mine_t), jnp.where(swap, mine_t, other_t)], 0
        )
        if base is not None:
            result = rest[0][...].astype(F32) - result
        copies = rest[-1]
        result = result.astype(BF16)
        for i in range(targets):
            copies[i] = result

    operands = (whole, mine, other) + (() if base is None else (base,))
    return pl.pallas_call(
        kernel,
        out_shape=jax.ShapeDtypeStruct((targets,) + whole.shape[1:], BF16),
        in_specs=[VMEM] * len(operands),
        out_specs=VMEM,
        compiler_params=PARAMS,
        name="back_step",
    )(*operands)


def join_kernel(mine, other, above, sample):
    core = lax.axis_index("core")
    half = mine.shape[1] // 2
    panels = 4
    here = pl.ds(pl.multiple_of(core * half, half), half)
    there = pl.ds(pl.multiple_of((1 - core) * half, half), half)
    for z in range(mine.shape[0] // panels):
        for c in range(2):
            for p in range(panels):
                at = z * 2 * panels + c * panels + p
                above[at, here] = mine[z * panels + p, c * half : (c + 1) * half]
                above[at, there] = other[z * panels + p, c * half : (c + 1) * half]
    own = lax.axis_index("pair") * 2 * panels + core * panels + lax.axis_index("panel")
    sample[...] = above[own].astype(F32).T.astype(BF16)


def join_halves(mine, other):
    return pl.pallas_call(
        join_kernel,
        out_shape=(
            jax.ShapeDtypeStruct((2 * mine.shape[0],) + mine.shape[1:], BF16),
            jax.ShapeDtypeStruct(mine.shape[1:], BF16),
        ),
        in_specs=[VMEM] * 2,
        out_specs=(VMEM,) * 2,
        compiler_params=PARAMS,
        name="join_halves",
    )(mine, other)


def leaf_backward_kernel(
    rows, count, whole, second, panels, inverse, solved_t, sample, sample1, first
):
    slots, touched, width = panels.shape[:3]
    half = width // 2
    split = whole.shape[0]
    line = split // 2
    for c in range(2):
        for p in range(line):
            for h in range(2):
                first[c * line + p, h * half : (h + 1) * half] = whole[
                    h * line + p, c * half : (c + 1) * half
                ]
    for s in range(slots):
        picked = []
        for k in range(touched):
            row = rows[s, k]
            low = first[jnp.minimum(row, split - 1)]
            high = second[jnp.maximum(row - split, 0)]
            picked.append(jnp.where(row < split, low, high))
        correction = dot(
            jnp.concatenate(picked, 1), panels[s].reshape(touched * width, width)
        )
        shifted = (solved_t[s].astype(F32) - correction).astype(BF16)
        live = jnp.where(s < count[0, 0], 1.0, 0.0)
        result = dot(shifted, inverse[s]) * live
        sample[s] = result.T.astype(BF16)
    own = lax.axis_index("core") * line + lax.axis_index("panel")
    sample1[...] = first[own].astype(F32).T.astype(BF16)


def leaf_backward(rows, count, whole, second, panels, inverse, solved_t):
    return pl.pallas_call(
        leaf_backward_kernel,
        out_shape=(
            jax.ShapeDtypeStruct(solved_t.shape, BF16),
            jax.ShapeDtypeStruct(whole.shape[1:], BF16),
        ),
        in_specs=[SMEM, SMEM] + [VMEM] * 5,
        out_specs=(VMEM,) * 2,
        scratch_shapes=[pltpu.VMEM(whole.shape, BF16)],
        compiler_params=PARAMS,
        name="leaf_backward",
    )(rows, count, whole, second, panels, inverse, solved_t)


def exchange(blocks, axes):
    return lax.all_to_all(blocks, axes, 0, 0, tiled=True)


def swapped(array):
    return lax.ppermute(array, "core", [(0, 1), (1, 0)])


def body(
    leaf_rhs,
    leaf_inverse,
    leaf_panel,
    panel_rows,
    live_count,
    sep1_rhs,
    sep1_inverse,
    sep1_panel,
    sep2_rhs,
    sep2_inverse,
):
    inverse, panels, rows = leaf_inverse[0, 0], leaf_panel[0, 0], panel_rows[0, 0]
    inverse1, inverse2, panel1 = sep1_inverse[0, 0], sep2_inverse[0, 0], sep1_panel[0, 0]
    width = inverse.shape[1]
    first_blocks = inverse1.shape[0] // width
    second_blocks = inverse2.shape[0] // width
    line = first_blocks // 2

    solved, send1, above = leaf_forward(
        rows,
        live_count,
        leaf_rhs[0, 0],
        inverse,
        panels,
        sep1_rhs[0, 0],
        first_blocks,
        second_blocks,
    )
    received1 = exchange(send1, FIRST)
    store, keep, solved_t, panels, inverse = leaf_second(
        above, solved, sep2_rhs[0, 0], inverse1, panel1, inverse2, panels, inverse
    )
    other = swapped(store)
    rows1, rows2 = inverse1.shape[0], inverse2.shape[0]
    panel1_at, inverse2_at, terms_at = rows1, rows1 + rows2, rows1 + 2 * rows2

    partial1 = side_partials(received1, store, other, 0, rows1)
    raised, solved1_t = raise_terms(
        exchange(partial1, LINE), keep, store, other, panel1_at, rows2, terms_at
    )
    partial2 = side_partials(exchange(raised, CHIPS), store, other, inverse2_at, rows2)
    whole_solved = exchange(turned_sum(exchange(partial2, CHIPS)), CHIPS)

    whole_second = exchange(
        back_step(whole_solved, store, other, inverse2_at, second_blocks // 2), CHIPS
    )
    shifted = back_step(whole_second, store, other, panel1_at, line, solved1_t)
    whole_shifted = exchange(shifted, LINE)
    other_second = swapped(lax.optimization_barrier((whole_second, shifted))[0])
    second, sample2 = join_halves(whole_second, other_second)
    whole_first = exchange(back_step(whole_shifted, store, other, 0, first_blocks), FIRST)
    leaf_sample, sample1 = leaf_backward(
        rows, live_count, whole_first, second, panels, inverse, solved_t
    )
    return (leaf_sample[None, None], sample1[None, None], sample2[None, None])


def solution(mesh):
    places = mesh.devices.reshape(-1, 2, 2, mesh.shape["panel"])
    fine = Mesh(places, ("group", "pair", "core", "panel"))
    leaf = ("group", "pair", "core")

    def spec(rank):
        return P("panel", leaf, *(None,) * (rank - 2))

    return jax.shard_map(
        body,
        mesh=fine,
        in_specs=tuple(spec(rank) for rank in (5, 5, 6, 4, 2, 4, 4, 4, 4, 4)),
        out_specs=tuple(spec(rank) for rank in (5, 4, 4)),
        check_vma=False,
    )
```

```python
import jax
import jax.numpy as jnp
from jax import lax
from jax.experimental import pallas as pl
from jax.experimental.pallas import tpu as pltpu
from jax.sharding import Mesh, PartitionSpec as P

FIRST = ("core", "panel")
CHIPS = ("pair", "panel")
LINE = ("panel",)
F32, BF16 = jnp.float32, jnp.bfloat16
VMEM = pl.BlockSpec(memory_space=pltpu.VMEM)
SMEM = pl.BlockSpec(memory_space=pltpu.SMEM)
HBM = pl.BlockSpec(memory_space=pltpu.HBM)
PARAMS = pltpu.CompilerParams(vmem_limit_bytes=24 << 20)


def in_hbm(*arrays):
    return [pltpu.with_memory_space_constraint(array, pltpu.HBM) for array in arrays]


def dot(left, right):
    return lax.dot_general(left, right, (((1,), (0,)), ((), ())), preferred_element_type=F32)


def half_lanes(block):
    return lax.broadcasted_iota(jnp.int32, block.shape, 1) < block.shape[1] // 2


def turned(block):
    return pltpu.roll(block, block.shape[1] // 2, 1)


def packed(lower, upper):
    low = half_lanes(lower)
    return jnp.where(low, lower, turned(upper)), jnp.where(low, turned(lower), upper)


def start_loads(sems, *pairs):
    loads = [pltpu.make_async_copy(*pair, sems.at[i]) for i, pair in enumerate(pairs)]
    for load in loads:
        load.start()
    return loads


def leaf_solve(count, inverse, rhs, slot):
    live = jnp.where(slot < count[0, 0], 1.0, 0.0)
    return (dot(inverse[slot], rhs[slot]) * live).astype(BF16)


def leaf_forward_kernel(
    rows_h,
    count,
    rhs,
    inverse,
    panels,
    side1,
    side2,
    inverse1,
    panel1,
    inverse2,
    send,
    store,
    keep,
    total,
    rows,
    rhs_v,
    inverse_v,
    panels_v,
    side1_v,
    side2_v,
    sems,
):
    rows1, rows2 = inverse1.shape[0], inverse2.shape[0]
    loads = start_loads(
        sems,
        (inverse, inverse_v),
        (rhs, rhs_v),
        (panels, panels_v),
        (rows_h, rows),
        (side1, side1_v),
        (side2, side2_v),
        (inverse1, store.at[0:rows1]),
        (panel1, store.at[rows1 : rows1 + rows2]),
        (inverse2, store.at[rows1 + rows2 : rows1 + 2 * rows2]),
    )
    slots, touched, width = panels_v.shape[:3]
    split = send.shape[0]
    line = split // 2
    core = lax.axis_index("core")
    total[...] = jnp.zeros_like(total)
    loads[0].wait()
    loads[1].wait()
    solved = [leaf_solve(count, inverse_v, rhs_v, s) for s in range(slots)]
    loads[2].wait()
    loads[3].wait()
    for s in range(slots):
        products = dot(panels_v[s].reshape(touched * width, width), solved[s])
        for k in range(touched):
            total[rows[s, k]] += products[k * width : (k + 1) * width]
    loads[4].wait()
    loads[5].wait()
    own = core * line + lax.axis_index("panel")
    total[own] -= side1_v[...].astype(F32)
    total[split + lax.axis_index("pair") * split + own] -= side2_v[...].astype(F32)
    for p in range(line):
        zero, one = packed(total[p], total[line + p])
        send[p] = zero.astype(BF16)
        send[line + p] = one.astype(BF16)
    away_row = rows1 + 2 * rows2
    for z in range(2):
        for p in range(line):
            at = split + z * split + p
            zero, one = packed(total[at], total[at + line])
            at = z * line + p
            keep[at] = jnp.where(core == 0, zero, one)
            away = jnp.where(core == 0, one, zero)
            store[away_row + at * width : away_row + (at + 1) * width] = away.astype(BF16)
    for load in loads[6:]:
        load.wait()


def leaf_forward(count, rows, rhs, inverse, panels, side1, side2, inverse1, panel1, inverse2):
    block = rhs.shape[1:]
    first_blocks, second_blocks = (m.shape[0] // block[0] for m in (inverse1, inverse2))
    halves = second_blocks // 2
    store_rows = inverse1.shape[0] + 2 * inverse2.shape[0] + halves * block[0]
    arrays = in_hbm(rhs, inverse, panels, side1, side2, inverse1, panel1, inverse2)
    return pl.pallas_call(
        leaf_forward_kernel,
        out_shape=(
            jax.ShapeDtypeStruct((first_blocks,) + block, BF16),
            jax.ShapeDtypeStruct((store_rows, block[0]), BF16),
            jax.ShapeDtypeStruct((halves,) + block, F32),
        ),
        in_specs=[HBM, SMEM] + [HBM] * len(arrays),
        out_specs=(VMEM,) * 3,
        scratch_shapes=[
            pltpu.VMEM((first_blocks + second_blocks,) + block, F32),
            pltpu.SMEM(rows.shape, rows.dtype),
            pltpu.VMEM(rhs.shape, BF16),
            pltpu.VMEM(inverse.shape, BF16),
            pltpu.VMEM(panels.shape, BF16),
            pltpu.VMEM(side1.shape, BF16),
            pltpu.VMEM(side2.shape, BF16),
            pltpu.SemaphoreType.DMA((9,)),
        ],
        compiler_params=PARAMS,
        name="leaf_forward",
    )(*in_hbm(rows), count, *arrays)


def column_products(piece, mine, other, first_row, row_count):
    low = half_lanes(piece)
    across = turned(piece)
    zero = jnp.zeros_like(piece)
    lower = (jnp.where(low, piece, zero), jnp.where(low, across, zero))
    upper = (jnp.where(low, zero, across), jnp.where(low, zero, piece))
    swap = lax.axis_index("core") == 1

    def ordered(two):
        return [jnp.where(swap, two[1], two[0]), jnp.where(swap, two[0], two[1])]

    weights = jnp.concatenate(ordered(lower) + ordered(upper), 0).astype(BF16)
    half = mine.shape[1] * 4
    parts = []
    for start in range(first_row, first_row + row_count, 2 * half):
        middle = start + half
        wide = jnp.concatenate(
            [
                mine[start:middle],
                other[start:middle],
                mine[middle : middle + half],
                other[middle : middle + half],
            ],
            1,
        )
        parts.append(dot(wide, weights))
    return parts


def side_partials(received, mine, other, first_row, row_count):
    width = mine.shape[1]

    def kernel(received, mine, other, partials):
        side = -received[...].astype(F32).sum(axis=0)
        side = side.astype(BF16).astype(F32)
        for z, part in enumerate(column_products(side, mine, other, first_row, row_count)):
            for p in range(4):
                partials[z * 4 + p] = part[p * width : (p + 1) * width].astype(BF16)

    return pl.pallas_call(
        kernel,
        out_shape=jax.ShapeDtypeStruct((row_count // width // 2,) + received.shape[1:], BF16),
        in_specs=[VMEM] * 3,
        out_specs=VMEM,
        compiler_params=PARAMS,
        name="side_partials",
    )(received, mine, other)


def raise_terms(received, keep, mine, other, first_row, row_count, terms_row):
    width = mine.shape[1]

    def kernel(received, keep, mine, other, raised, solved_t):
        piece = received[...].astype(F32).sum(axis=0)
        piece = piece.astype(BF16).astype(F32)
        for z, part in enumerate(column_products(piece, mine, other, first_row, row_count)):
            for p in range(4):
                at = z * 4 + p
                came = other[terms_row + at * width : terms_row + (at + 1) * width]
                terms = keep[at] + came.astype(F32)
                raised[at] = (part[p * width : (p + 1) * width] + terms).astype(BF16)
        solved_t[...] = piece.T.astype(BF16)

    return pl.pallas_call(
        kernel,
        out_shape=(
            jax.ShapeDtypeStruct(keep.shape, BF16),
            jax.ShapeDtypeStruct(received.shape[1:], BF16),
        ),
        in_specs=[VMEM] * 4,
        out_specs=(VMEM,) * 2,
        compiler_params=PARAMS,
        name="raise_terms",
    )(received, keep, mine, other)


def turn_kernel(received, copies):
    piece = received[...].astype(F32).sum(axis=0).T.astype(BF16)
    for i in range(copies.shape[0]):
        copies[i] = piece


def turned_sum(received):
    return pl.pallas_call(
        turn_kernel,
        out_shape=jax.ShapeDtypeStruct(received.shape, BF16),
        in_specs=[VMEM],
        out_specs=VMEM,
        compiler_params=PARAMS,
        name="turned_sum",
    )(received)


def back_step(whole, mine, other, first_row, targets, base=None):
    panels = 4
    half = whole.shape[1] // 2
    rows = pl.ds(first_row, 2 * whole.shape[0] * mine.shape[1])

    def kernel(whole, mine, other, *rest):
        pieces = []
        for z in range(whole.shape[0] // panels):
            for c in range(2):
                for p in range(panels):
                    pieces.append(whole[z * panels + p, c * half : (c + 1) * half])
        vectors = jnp.concatenate(pieces, 1)
        mine_t = dot(vectors, mine[rows])
        other_t = dot(vectors, other[rows])
        swap = lax.axis_index("core") == 1
        result = jnp.concatenate(
            [jnp.where(swap, other_t, mine_t), jnp.where(swap, mine_t, other_t)], 0
        )
        if base is not None:
            result = rest[0][...].astype(F32) - result
        copies = rest[-1]
        result = result.astype(BF16)
        for i in range(targets):
            copies[i] = result

    operands = (whole, mine, other) + (() if base is None else (base,))
    return pl.pallas_call(
        kernel,
        out_shape=jax.ShapeDtypeStruct((targets,) + whole.shape[1:], BF16),
        in_specs=[VMEM] * len(operands),
        out_specs=VMEM,
        compiler_params=PARAMS,
        name="back_step",
    )(*operands)


def reload_kernel(count, rhs, inverse, panels, inverse_v, panels_v, solved_t, rhs_v, sems):
    loads = start_loads(sems, (inverse, inverse_v), (rhs, rhs_v), (panels, panels_v))
    loads[0].wait()
    loads[1].wait()
    for s in range(solved_t.shape[0]):
        solved_t[s] = leaf_solve(count, inverse_v, rhs_v, s).astype(F32).T.astype(BF16)
    loads[2].wait()


def leaf_reload(count, rhs, inverse, panels):
    return pl.pallas_call(
        reload_kernel,
        out_shape=tuple(jax.ShapeDtypeStruct(a.shape, BF16) for a in (inverse, panels, rhs)),
        in_specs=[SMEM] + [HBM] * 3,
        out_specs=(VMEM,) * 3,
        scratch_shapes=[pltpu.VMEM(rhs.shape, BF16), pltpu.SemaphoreType.DMA((3,))],
        compiler_params=PARAMS,
        name="leaf_reload",
    )(count, *in_hbm(rhs, inverse, panels))


def leaf_backward_kernel(
    rows, count, whole, mine, other, panels, inverse, solved_t, sample, sample1, sample2
):
    slots, touched, width = panels.shape[:3]
    half = width // 2
    line = 4
    split = 2 * line
    core = lax.axis_index("core")

    def first_block(block):
        at = pl.ds(pl.multiple_of(block // line * half, half), half)
        return [whole[h * line + block % line, at] for h in range(2)]

    def second_block(block):
        at = pl.ds(pl.multiple_of(block // line % 2 * half, half), half)
        place = block // split * line + block % line
        here, there = mine[place, at], other[place, at]
        return [jnp.where(core == 0, here, there), jnp.where(core == 0, there, here)]

    for s in range(slots):
        picked = []
        for k in range(touched):
            row = rows[s, k]
            low = first_block(jnp.minimum(row, split - 1))
            high = second_block(jnp.maximum(row - split, 0))
            chosen = [jnp.where(row < split, a, b) for a, b in zip(low, high)]
            picked.append(jnp.concatenate(chosen, 0))
        correction = dot(
            jnp.concatenate(picked, 1), panels[s].reshape(touched * width, width)
        )
        shifted = (solved_t[s].astype(F32) - correction).astype(BF16)
        live = jnp.where(s < count[0, 0], 1.0, 0.0)
        result = dot(shifted, inverse[s]) * live
        sample[s] = result.T.astype(BF16)
    own = core * line + lax.axis_index("panel")
    sample1[...] = jnp.concatenate(first_block(own), 0).astype(F32).T.astype(BF16)
    own = own + lax.axis_index("pair") * split
    sample2[...] = jnp.concatenate(second_block(own), 0).astype(F32).T.astype(BF16)


def leaf_backward(rows, count, whole, mine, other, panels, inverse, solved_t):
    return pl.pallas_call(
        leaf_backward_kernel,
        out_shape=(
            jax.ShapeDtypeStruct(solved_t.shape, BF16),
            jax.ShapeDtypeStruct(whole.shape[1:], BF16),
            jax.ShapeDtypeStruct(whole.shape[1:], BF16),
        ),
        in_specs=[SMEM, SMEM] + [VMEM] * 6,
        out_specs=(VMEM,) * 3,
        compiler_params=PARAMS,
        name="leaf_backward",
    )(rows, count, whole, mine, other, panels, inverse, solved_t)


def exchange(blocks, axes):
    return lax.all_to_all(blocks, axes, 0, 0, tiled=True)


def swapped(array):
    return lax.ppermute(array, "core", [(0, 1), (1, 0)])


def body(
    leaf_rhs,
    leaf_inverse,
    leaf_panel,
    panel_rows,
    live_count,
    sep1_rhs,
    sep1_inverse,
    sep1_panel,
    sep2_rhs,
    sep2_inverse,
):
    rhs, inverse, panels = leaf_rhs[0, 0], leaf_inverse[0, 0], leaf_panel[0, 0]
    rows = panel_rows[0, 0]
    inverse1, inverse2, panel1 = sep1_inverse[0, 0], sep2_inverse[0, 0], sep1_panel[0, 0]
    width = inverse.shape[1]
    first_blocks = inverse1.shape[0] // width
    second_blocks = inverse2.shape[0] // width
    rows1, rows2 = inverse1.shape[0], inverse2.shape[0]
    panel1_at, inverse2_at, terms_at = rows1, rows1 + rows2, rows1 + 2 * rows2

    send1, store, keep = leaf_forward(
        live_count,
        rows,
        rhs,
        inverse,
        panels,
        sep1_rhs[0, 0],
        sep2_rhs[0, 0],
        inverse1,
        panel1,
        inverse2,
    )
    other = swapped(store)
    partial1 = side_partials(exchange(send1, FIRST), store, other, 0, rows1)
    raised, solved1_t = raise_terms(
        exchange(partial1, LINE), keep, store, other, panel1_at, rows2, terms_at
    )
    partial2 = side_partials(exchange(raised, CHIPS), store, other, inverse2_at, rows2)
    whole_solved = exchange(turned_sum(exchange(partial2, CHIPS)), CHIPS)

    whole_second = exchange(
        back_step(whole_solved, store, other, inverse2_at, second_blocks // 2), CHIPS
    )
    shifted = back_step(whole_second, store, other, panel1_at, first_blocks // 2, solved1_t)
    whole_shifted = exchange(shifted, LINE)
    second_late, rhs, inverse, panels, _ = lax.optimization_barrier(
        (whole_second, rhs, inverse, panels, shifted)
    )
    other_second = swapped(second_late)
    inverse, panels, solved_t = leaf_reload(live_count, rhs, inverse, panels)
    whole_shifted, inverse, panels, solved_t = lax.optimization_barrier(
        (whole_shifted, inverse, panels, solved_t)
    )
    whole_first = exchange(back_step(whole_shifted, store, other, 0, first_blocks), FIRST)
    leaf_sample, sample1, sample2 = leaf_backward(
        rows, live_count, whole_first, whole_second, other_second, panels, inverse, solved_t
    )
    return (leaf_sample[None, None], sample1[None, None], sample2[None, None])


def solution(mesh):
    places = mesh.devices.reshape(-1, 2, 2, mesh.shape["panel"])
    fine = Mesh(places, ("group", "pair", "core", "panel"))
    leaf = ("group", "pair", "core")

    def spec(rank):
        return P("panel", leaf, *(None,) * (rank - 2))

    return jax.shard_map(
        body,
        mesh=fine,
        in_specs=tuple(spec(rank) for rank in (5, 5, 6, 4, 2, 4, 4, 4, 4, 4)),
        out_specs=tuple(spec(rank) for rank in (5, 4, 4)),
        check_vma=False,
    )
```

```python
import jax
import jax.numpy as jnp
from jax import lax
from jax.experimental import pallas as pl
from jax.experimental.pallas import tpu as pltpu
from jax.sharding import Mesh, PartitionSpec as P

FIRST = ("core", "panel")
CHIPS = ("pair", "panel")
LINE = ("panel",)
F32, BF16 = jnp.float32, jnp.bfloat16
VMEM = pl.BlockSpec(memory_space=pltpu.VMEM)
SMEM = pl.BlockSpec(memory_space=pltpu.SMEM)
HBM = pl.BlockSpec(memory_space=pltpu.HBM)
PARAMS = pltpu.CompilerParams(vmem_limit_bytes=24 << 20)


def in_hbm(*arrays):
    return [pltpu.with_memory_space_constraint(array, pltpu.HBM) for array in arrays]


def dot(left, right):
    return lax.dot_general(left, right, (((1,), (0,)), ((), ())), preferred_element_type=F32)


def half_lanes(block):
    return lax.broadcasted_iota(jnp.int32, block.shape, 1) < block.shape[1] // 2


def turned(block):
    return pltpu.roll(block, block.shape[1] // 2, 1)


def packed(lower, upper):
    low = half_lanes(lower)
    return jnp.where(low, lower, turned(upper)), jnp.where(low, turned(lower), upper)


def start_loads(sems, *pairs):
    loads = [pltpu.make_async_copy(*pair, sems.at[i]) for i, pair in enumerate(pairs)]
    for load in loads:
        load.start()
    return loads


def leaf_solve(count, inverse, rhs, slot):
    live = jnp.where(slot < count[0, 0], 1.0, 0.0)
    return (dot(inverse[slot], rhs[slot]) * live).astype(BF16)


def leaf_forward_kernel(
    rows_h,
    count,
    rhs,
    inverse,
    panels,
    side1,
    side2,
    inverse1,
    panel1,
    inverse2,
    send,
    store,
    keep,
    total,
    rows,
    rhs_v,
    inverse_v,
    panels_v,
    side1_v,
    side2_v,
    sems,
):
    rows1, rows2 = inverse1.shape[0], inverse2.shape[0]
    loads = start_loads(
        sems,
        (inverse, inverse_v),
        (rhs, rhs_v),
        (panels, panels_v),
        (rows_h, rows),
        (side1, side1_v),
        (side2, side2_v),
        (inverse1, store.at[0:rows1]),
        (panel1, store.at[rows1 : rows1 + rows2]),
        (inverse2, store.at[rows1 + rows2 : rows1 + 2 * rows2]),
    )
    slots, touched, width = panels_v.shape[:3]
    split = send.shape[0]
    line = split // 2
    core = lax.axis_index("core")
    total[...] = jnp.zeros_like(total)
    loads[0].wait()
    loads[1].wait()
    solved = [leaf_solve(count, inverse_v, rhs_v, s) for s in range(slots)]
    loads[2].wait()
    loads[3].wait()
    for s in range(slots):
        products = dot(panels_v[s].reshape(touched * width, width), solved[s])
        for k in range(touched):
            total[rows[s, k]] += products[k * width : (k + 1) * width]
    loads[4].wait()
    loads[5].wait()
    own = core * line + lax.axis_index("panel")
    total[own] -= side1_v[...].astype(F32)
    total[split + lax.axis_index("pair") * split + own] -= side2_v[...].astype(F32)
    for p in range(line):
        zero, one = packed(total[p], total[line + p])
        send[p] = zero.astype(BF16)
        send[line + p] = one.astype(BF16)
    away_row = rows1 + 2 * rows2
    for z in range(2):
        for p in range(line):
            at = split + z * split + p
            zero, one = packed(total[at], total[at + line])
            at = z * line + p
            keep[at] = jnp.where(core == 0, zero, one)
            away = jnp.where(core == 0, one, zero)
            store[away_row + at * width : away_row + (at + 1) * width] = away.astype(BF16)
    for load in loads[6:]:
        load.wait()


def leaf_forward(count, rows, rhs, inverse, panels, side1, side2, inverse1, panel1, inverse2):
    block = rhs.shape[1:]
    first_blocks, second_blocks = (m.shape[0] // block[0] for m in (inverse1, inverse2))
    halves = second_blocks // 2
    store_rows = inverse1.shape[0] + 2 * inverse2.shape[0] + halves * block[0]
    arrays = in_hbm(rhs, inverse, panels, side1, side2, inverse1, panel1, inverse2)
    return pl.pallas_call(
        leaf_forward_kernel,
        out_shape=(
            jax.ShapeDtypeStruct((first_blocks,) + block, BF16),
            jax.ShapeDtypeStruct((store_rows, block[0]), BF16),
            jax.ShapeDtypeStruct((halves,) + block, F32),
        ),
        in_specs=[HBM, SMEM] + [HBM] * len(arrays),
        out_specs=(VMEM,) * 3,
        scratch_shapes=[
            pltpu.VMEM((first_blocks + second_blocks,) + block, F32),
            pltpu.SMEM(rows.shape, rows.dtype),
            pltpu.VMEM(rhs.shape, BF16),
            pltpu.VMEM(inverse.shape, BF16),
            pltpu.VMEM(panels.shape, BF16),
            pltpu.VMEM(side1.shape, BF16),
            pltpu.VMEM(side2.shape, BF16),
            pltpu.SemaphoreType.DMA((9,)),
        ],
        compiler_params=PARAMS,
        name="leaf_forward",
    )(*in_hbm(rows), count, *arrays)


def column_products(piece, mine, other, first_row, row_count):
    low = half_lanes(piece)
    across = turned(piece)
    zero = jnp.zeros_like(piece)
    lower = (jnp.where(low, piece, zero), jnp.where(low, across, zero))
    upper = (jnp.where(low, zero, across), jnp.where(low, zero, piece))
    swap = lax.axis_index("core") == 1

    def ordered(two):
        return [jnp.where(swap, two[1], two[0]), jnp.where(swap, two[0], two[1])]

    weights = jnp.concatenate(ordered(lower) + ordered(upper), 0).astype(BF16)
    half = mine.shape[1] * 4
    parts = []
    for start in range(first_row, first_row + row_count, 2 * half):
        middle = start + half
        wide = jnp.concatenate(
            [
                mine[start:middle],
                other[start:middle],
                mine[middle : middle + half],
                other[middle : middle + half],
            ],
            1,
        )
        parts.append(dot(wide, weights))
    return parts


def side_partials(received, mine, other, first_row, row_count):
    width = mine.shape[1]

    def kernel(received, mine, other, partials):
        side = -received[...].astype(F32).sum(axis=0)
        side = side.astype(BF16).astype(F32)
        for z, part in enumerate(column_products(side, mine, other, first_row, row_count)):
            for p in range(4):
                partials[z * 4 + p] = part[p * width : (p + 1) * width].astype(BF16)

    return pl.pallas_call(
        kernel,
        out_shape=jax.ShapeDtypeStruct((row_count // width // 2,) + received.shape[1:], BF16),
        in_specs=[VMEM] * 3,
        out_specs=VMEM,
        compiler_params=PARAMS,
        name="side_partials",
    )(received, mine, other)


def raise_terms(received, keep, mine, other, first_row, row_count, terms_row):
    width = mine.shape[1]

    def kernel(received, keep, mine, other, raised, solved_t):
        piece = received[...].astype(F32).sum(axis=0)
        piece = piece.astype(BF16).astype(F32)
        for z, part in enumerate(column_products(piece, mine, other, first_row, row_count)):
            for p in range(4):
                at = z * 4 + p
                came = other[terms_row + at * width : terms_row + (at + 1) * width]
                terms = keep[at] + came.astype(F32)
                raised[at] = (part[p * width : (p + 1) * width] + terms).astype(BF16)
        solved_t[...] = piece.T.astype(BF16)

    return pl.pallas_call(
        kernel,
        out_shape=(
            jax.ShapeDtypeStruct(keep.shape, BF16),
            jax.ShapeDtypeStruct(received.shape[1:], BF16),
        ),
        in_specs=[VMEM] * 4,
        out_specs=(VMEM,) * 2,
        compiler_params=PARAMS,
        name="raise_terms",
    )(received, keep, mine, other)


def turn_kernel(received, copies):
    piece = received[...].astype(F32).sum(axis=0).T.astype(BF16)
    for i in range(copies.shape[0]):
        copies[i] = piece


def turned_sum(received):
    return pl.pallas_call(
        turn_kernel,
        out_shape=jax.ShapeDtypeStruct(received.shape, BF16),
        in_specs=[VMEM],
        out_specs=VMEM,
        compiler_params=PARAMS,
        name="turned_sum",
    )(received)


def back_step(whole, mine, other, first_row, targets, base=None):
    panels = 4
    half = whole.shape[1] // 2
    rows = pl.ds(first_row, 2 * whole.shape[0] * mine.shape[1])

    def kernel(whole, mine, other, *rest):
        pieces = []
        for z in range(whole.shape[0] // panels):
            for c in range(2):
                for p in range(panels):
                    pieces.append(whole[z * panels + p, c * half : (c + 1) * half])
        vectors = jnp.concatenate(pieces, 1)
        mine_t = dot(vectors, mine[rows])
        other_t = dot(vectors, other[rows])
        swap = lax.axis_index("core") == 1
        result = jnp.concatenate(
            [jnp.where(swap, other_t, mine_t), jnp.where(swap, mine_t, other_t)], 0
        )
        if base is not None:
            result = rest[0][...].astype(F32) - result
        copies = rest[-1]
        result = result.astype(BF16)
        for i in range(targets):
            copies[i] = result

    operands = (whole, mine, other) + (() if base is None else (base,))
    return pl.pallas_call(
        kernel,
        out_shape=jax.ShapeDtypeStruct((targets,) + whole.shape[1:], BF16),
        in_specs=[VMEM] * len(operands),
        out_specs=VMEM,
        compiler_params=PARAMS,
        name="back_step",
    )(*operands)


def leaf_backward_kernel(
    rows,
    count,
    rhs,
    inverse,
    panels,
    whole,
    mine,
    other,
    sample,
    sample1,
    sample2,
    rhs_v,
    inverse_v,
    panels_v,
    picked,
    sems,
):
    loads = start_loads(sems, (inverse, inverse_v), (rhs, rhs_v), (panels, panels_v))
    slots, touched, width = panels_v.shape[:3]
    half = width // 2
    line = 4
    split = 2 * line
    core = lax.axis_index("core")

    def first_block(block):
        at = pl.ds(pl.multiple_of(block // line * half, half), half)
        return [whole[h * line + block % line, at] for h in range(2)]

    def second_block(block):
        at = pl.ds(pl.multiple_of(block // line % 2 * half, half), half)
        place = block // split * line + block % line
        here, there = mine[place, at], other[place, at]
        return [jnp.where(core == 0, here, there), jnp.where(core == 0, there, here)]

    for s in range(slots):
        for k in range(touched):
            row = rows[s, k]
            low = first_block(jnp.minimum(row, split - 1))
            high = second_block(jnp.maximum(row - split, 0))
            for h in range(2):
                picked[s, h * half : (h + 1) * half, k * width : (k + 1) * width] = jnp.where(
                    row < split, low[h], high[h]
                )
    own = core * line + lax.axis_index("panel")
    sample1[...] = jnp.concatenate(first_block(own), 0).astype(F32).T.astype(BF16)
    own = own + lax.axis_index("pair") * split
    sample2[...] = jnp.concatenate(second_block(own), 0).astype(F32).T.astype(BF16)
    loads[0].wait()
    loads[1].wait()
    solved_t = [
        leaf_solve(count, inverse_v, rhs_v, s).astype(F32).T for s in range(slots)
    ]
    loads[2].wait()
    for s in range(slots):
        correction = dot(picked[s], panels_v[s].reshape(touched * width, width))
        shifted = (solved_t[s] - correction).astype(BF16)
        live = jnp.where(s < count[0, 0], 1.0, 0.0)
        result = dot(shifted, inverse_v[s]) * live
        sample[s] = result.T.astype(BF16)


def leaf_backward(rows, count, rhs, inverse, panels, whole, mine, other):
    slots, touched, width = panels.shape[:3]
    block = jax.ShapeDtypeStruct(whole.shape[1:], BF16)
    return pl.pallas_call(
        leaf_backward_kernel,
        out_shape=(jax.ShapeDtypeStruct(rhs.shape, BF16), block, block),
        in_specs=[SMEM, SMEM] + [HBM] * 3 + [VMEM] * 3,
        out_specs=(VMEM,) * 3,
        scratch_shapes=[
            pltpu.VMEM(rhs.shape, BF16),
            pltpu.VMEM(inverse.shape, BF16),
            pltpu.VMEM(panels.shape, BF16),
            pltpu.VMEM((slots, whole.shape[1], touched * width), BF16),
            pltpu.SemaphoreType.DMA((3,)),
        ],
        compiler_params=PARAMS,
        name="leaf_backward",
    )(rows, count, *in_hbm(rhs, inverse, panels), whole, mine, other)


def exchange(blocks, axes):
    return lax.all_to_all(blocks, axes, 0, 0, tiled=True)


def swapped(array):
    return lax.ppermute(array, "core", [(0, 1), (1, 0)])


def body(
    leaf_rhs,
    leaf_inverse,
    leaf_panel,
    panel_rows,
    live_count,
    sep1_rhs,
    sep1_inverse,
    sep1_panel,
    sep2_rhs,
    sep2_inverse,
):
    rhs, inverse, panels = leaf_rhs[0, 0], leaf_inverse[0, 0], leaf_panel[0, 0]
    rows = panel_rows[0, 0]
    inverse1, inverse2, panel1 = sep1_inverse[0, 0], sep2_inverse[0, 0], sep1_panel[0, 0]
    width = inverse.shape[1]
    first_blocks = inverse1.shape[0] // width
    second_blocks = inverse2.shape[0] // width
    rows1, rows2 = inverse1.shape[0], inverse2.shape[0]
    panel1_at, inverse2_at, terms_at = rows1, rows1 + rows2, rows1 + 2 * rows2

    send1, store, keep = leaf_forward(
        live_count,
        rows,
        rhs,
        inverse,
        panels,
        sep1_rhs[0, 0],
        sep2_rhs[0, 0],
        inverse1,
        panel1,
        inverse2,
    )
    other = swapped(store)
    partial1 = side_partials(exchange(send1, FIRST), store, other, 0, rows1)
    raised, solved1_t = raise_terms(
        exchange(partial1, LINE), keep, store, other, panel1_at, rows2, terms_at
    )
    partial2 = side_partials(exchange(raised, CHIPS), store, other, inverse2_at, rows2)
    whole_solved = exchange(turned_sum(exchange(partial2, CHIPS)), CHIPS)

    whole_second = exchange(
        back_step(whole_solved, store, other, inverse2_at, second_blocks // 2), CHIPS
    )
    shifted = back_step(whole_second, store, other, panel1_at, first_blocks // 2, solved1_t)
    whole_shifted = exchange(shifted, LINE)
    other_second = swapped(lax.optimization_barrier((whole_second, shifted))[0])
    whole_shifted, other_second = lax.optimization_barrier((whole_shifted, other_second))
    whole_first = exchange(back_step(whole_shifted, store, other, 0, first_blocks), FIRST)
    leaf_sample, sample1, sample2 = leaf_backward(
        rows, live_count, rhs, inverse, panels, whole_first, whole_second, other_second
    )
    return (leaf_sample[None, None], sample1[None, None], sample2[None, None])


def solution(mesh):
    places = mesh.devices.reshape(-1, 2, 2, mesh.shape["panel"])
    fine = Mesh(places, ("group", "pair", "core", "panel"))
    leaf = ("group", "pair", "core")

    def spec(rank):
        return P("panel", leaf, *(None,) * (rank - 2))

    return jax.shard_map(
        body,
        mesh=fine,
        in_specs=tuple(spec(rank) for rank in (5, 5, 6, 4, 2, 4, 4, 4, 4, 4)),
        out_specs=tuple(spec(rank) for rank in (5, 4, 4)),
        check_vma=False,
    )
```

```python
import jax
import jax.numpy as jnp
from jax import lax
from jax.experimental import pallas as pl
from jax.experimental.pallas import tpu as pltpu
from jax.sharding import Mesh, PartitionSpec as P

FIRST = ("core", "panel")
CHIPS = ("pair", "panel")
LINE = ("panel",)
F32, BF16 = jnp.float32, jnp.bfloat16
VMEM = pl.BlockSpec(memory_space=pltpu.VMEM)
SMEM = pl.BlockSpec(memory_space=pltpu.SMEM)
HBM = pl.BlockSpec(memory_space=pltpu.HBM)
PARAMS = pltpu.CompilerParams(vmem_limit_bytes=24 << 20)


def in_hbm(*arrays):
    return [pltpu.with_memory_space_constraint(array, pltpu.HBM) for array in arrays]


def dot(left, right):
    return lax.dot_general(left, right, (((1,), (0,)), ((), ())), preferred_element_type=F32)


def half_lanes(block):
    return lax.broadcasted_iota(jnp.int32, block.shape, 1) < block.shape[1] // 2


def turned(block):
    return pltpu.roll(block, block.shape[1] // 2, 1)


def packed(lower, upper):
    low = half_lanes(lower)
    return jnp.where(low, lower, turned(upper)), jnp.where(low, turned(lower), upper)


def start_loads(sems, *pairs):
    loads = [pltpu.make_async_copy(*pair, sems.at[i]) for i, pair in enumerate(pairs)]
    for load in loads:
        load.start()
    return loads


def store_rows(rows1, rows2, slots, touched, width):
    sizes = {
        "inverse1": rows1,
        "panel1": rows2,
        "inverse2": rows2,
        "terms": rows2 // 2,
        "panels": slots * touched * width,
        "inverse": slots * width,
        "solved": slots * width,
    }
    places, end = {}, 0
    for name, size in sizes.items():
        places[name] = end
        end += size
    return places, end


def leaf_forward(
    places, count, rows, rhs, inverse, panels, side1, side2, inverse1, panel1, inverse2
):
    block = rhs.shape[1:]
    width = block[0]
    slots, touched = rows.shape
    first_blocks, second_blocks = inverse1.shape[0] // width, inverse2.shape[0] // width
    halves, line = second_blocks // 2, first_blocks // 2
    own_rows, all_rows = places

    def kernel(
        rows_h,
        count,
        rhs,
        inverse,
        panels,
        side1,
        side2,
        inverse1,
        panel1,
        inverse2,
        send,
        store,
        keep,
        total,
        rows,
        rhs_v,
        side1_v,
        side2_v,
        sems,
        more_sems,
    ):
        def part(name, start=0, size=None, of=None):
            first = own_rows[name] + start
            return slice(first, first + (of.shape[0] if size is None else size))

        loads = start_loads(
            sems,
            (inverse, store.at[part("inverse", of=inverse)]),
            (rhs, rhs_v),
            (panels, store.at[part("panels", of=panels)]),
            (rows_h, rows),
            (side1, side1_v),
            (side2, side2_v),
        )
        core = lax.axis_index("core")
        total[...] = jnp.zeros_like(total)
        loads[0].wait()
        loads[1].wait()
        matrices = start_loads(
            more_sems,
            (inverse1, store.at[part("inverse1", of=inverse1)]),
            (panel1, store.at[part("panel1", of=panel1)]),
            (inverse2, store.at[part("inverse2", of=inverse2)]),
        )
        solved = []
        for s in range(slots):
            live = jnp.where(s < count[0, 0], 1.0, 0.0)
            piece = dot(store[part("inverse", s * width, width)], rhs_v[s]) * live
            piece = piece.astype(BF16)
            store[part("solved", s * width, width)] = piece.astype(F32).T.astype(BF16)
            solved.append(piece)
        loads[2].wait()
        loads[3].wait()
        for s in range(slots):
            tall = touched * width
            products = dot(store[part("panels", s * tall, tall)], solved[s])
            for k in range(touched):
                total[rows[s, k]] += products[k * width : (k + 1) * width]
        loads[4].wait()
        loads[5].wait()
        own = core * line + lax.axis_index("panel")
        total[own] -= side1_v[...].astype(F32)
        own = own + (lax.axis_index("pair") + 1) * first_blocks
        total[own] -= side2_v[...].astype(F32)
        for p in range(line):
            zero, one = packed(total[p], total[line + p])
            send[p] = zero.astype(BF16)
            send[line + p] = one.astype(BF16)
        for z in range(2):
            for p in range(line):
                at = (z + 1) * first_blocks + p
                zero, one = packed(total[at], total[at + line])
                at = z * line + p
                keep[at] = jnp.where(core == 0, zero, one)
                away = jnp.where(core == 0, one, zero)
                store[part("terms", at * width, width)] = away.astype(BF16)
        for load in matrices:
            load.wait()

    arrays = in_hbm(
        rhs,
        inverse.reshape(-1, width),
        panels.reshape(-1, width),
        side1,
        side2,
        inverse1,
        panel1,
        inverse2,
    )
    return pl.pallas_call(
        kernel,
        out_shape=(
            jax.ShapeDtypeStruct((first_blocks,) + block, BF16),
            jax.ShapeDtypeStruct((all_rows, width), BF16),
            jax.ShapeDtypeStruct((halves,) + block, F32),
        ),
        in_specs=[HBM, SMEM] + [HBM] * len(arrays),
        out_specs=(VMEM,) * 3,
        scratch_shapes=[
            pltpu.VMEM((first_blocks + second_blocks,) + block, F32),
            pltpu.SMEM(rows.shape, rows.dtype),
            pltpu.VMEM(rhs.shape, BF16),
            pltpu.VMEM(side1.shape, BF16),
            pltpu.VMEM(side2.shape, BF16),
            pltpu.SemaphoreType.DMA((6,)),
            pltpu.SemaphoreType.DMA((3,)),
        ],
        compiler_params=PARAMS,
        name="leaf_forward",
    )(*in_hbm(rows), count, *arrays)


def column_products(piece, mine, other, first_row, row_count):
    low = half_lanes(piece)
    across = turned(piece)
    zero = jnp.zeros_like(piece)
    lower = (jnp.where(low, piece, zero), jnp.where(low, across, zero))
    upper = (jnp.where(low, zero, across), jnp.where(low, zero, piece))
    swap = lax.axis_index("core") == 1

    def ordered(two):
        return [jnp.where(swap, two[1], two[0]), jnp.where(swap, two[0], two[1])]

    weights = jnp.concatenate(ordered(lower) + ordered(upper), 0).astype(BF16)
    half = mine.shape[1] * 4
    parts = []
    for start in range(first_row, first_row + row_count, 2 * half):
        middle = start + half
        wide = jnp.concatenate(
            [
                mine[start:middle],
                other[start:middle],
                mine[middle : middle + half],
                other[middle : middle + half],
            ],
            1,
        )
        parts.append(dot(wide, weights))
    return parts


def side_partials(received, mine, other, first_row, row_count):
    width = mine.shape[1]

    def kernel(received, mine, other, partials):
        side = -received[...].astype(F32).sum(axis=0)
        side = side.astype(BF16).astype(F32)
        for z, part in enumerate(column_products(side, mine, other, first_row, row_count)):
            for p in range(4):
                partials[z * 4 + p] = part[p * width : (p + 1) * width].astype(BF16)

    return pl.pallas_call(
        kernel,
        out_shape=jax.ShapeDtypeStruct((row_count // width // 2,) + received.shape[1:], BF16),
        in_specs=[VMEM] * 3,
        out_specs=VMEM,
        compiler_params=PARAMS,
        name="side_partials",
    )(received, mine, other)


def raise_terms(received, keep, mine, other, first_row, row_count, terms_row):
    width = mine.shape[1]

    def kernel(received, keep, mine, other, raised, solved_t):
        piece = received[...].astype(F32).sum(axis=0)
        piece = piece.astype(BF16).astype(F32)
        for z, part in enumerate(column_products(piece, mine, other, first_row, row_count)):
            for p in range(4):
                at = z * 4 + p
                came = other[terms_row + at * width : terms_row + (at + 1) * width]
                terms = keep[at] + came.astype(F32)
                raised[at] = (part[p * width : (p + 1) * width] + terms).astype(BF16)
        solved_t[...] = piece.T.astype(BF16)

    return pl.pallas_call(
        kernel,
        out_shape=(
            jax.ShapeDtypeStruct(keep.shape, BF16),
            jax.ShapeDtypeStruct(received.shape[1:], BF16),
        ),
        in_specs=[VMEM] * 4,
        out_specs=(VMEM,) * 2,
        compiler_params=PARAMS,
        name="raise_terms",
    )(received, keep, mine, other)


def turn_kernel(received, copies):
    piece = received[...].astype(F32).sum(axis=0).T.astype(BF16)
    for i in range(copies.shape[0]):
        copies[i] = piece


def turned_sum(received):
    return pl.pallas_call(
        turn_kernel,
        out_shape=jax.ShapeDtypeStruct(received.shape, BF16),
        in_specs=[VMEM],
        out_specs=VMEM,
        compiler_params=PARAMS,
        name="turned_sum",
    )(received)


def back_step(whole, mine, other, first_row, targets, base=None):
    panels = 4
    half = whole.shape[1] // 2
    rows = pl.ds(first_row, 2 * whole.shape[0] * mine.shape[1])

    def kernel(whole, mine, other, *rest):
        pieces = []
        for z in range(whole.shape[0] // panels):
            for c in range(2):
                for p in range(panels):
                    pieces.append(whole[z * panels + p, c * half : (c + 1) * half])
        vectors = jnp.concatenate(pieces, 1)
        mine_t = dot(vectors, mine[rows])
        other_t = dot(vectors, other[rows])
        swap = lax.axis_index("core") == 1
        result = jnp.concatenate(
            [jnp.where(swap, other_t, mine_t), jnp.where(swap, mine_t, other_t)], 0
        )
        if base is not None:
            result = rest[0][...].astype(F32) - result
        copies = rest[-1]
        result = result.astype(BF16)
        for i in range(targets):
            copies[i] = result

    operands = (whole, mine, other) + (() if base is None else (base,))
    return pl.pallas_call(
        kernel,
        out_shape=jax.ShapeDtypeStruct((targets,) + whole.shape[1:], BF16),
        in_specs=[VMEM] * len(operands),
        out_specs=VMEM,
        compiler_params=PARAMS,
        name="back_step",
    )(*operands)


def leaf_backward(places, rows, count, whole, mine, other, store):
    slots, touched = rows.shape
    width = whole.shape[1]
    half = width // 2
    split = whole.shape[0]
    line = split // 2
    own_rows, _ = places

    def kernel(rows, count, whole, mine, other, store, sample, sample1, sample2, above):
        core = lax.axis_index("core")
        here = pl.ds(pl.multiple_of(core * half, half), half)
        there = pl.ds(pl.multiple_of((1 - core) * half, half), half)
        for c in range(2):
            part = slice(c * half, (c + 1) * half)
            for p in range(line):
                for h in range(2):
                    above[c * line + p, h * half : (h + 1) * half] = whole[h * line + p, part]
                for z in range(2):
                    at = (z + 1) * split + c * line + p
                    above[at, here] = mine[z * line + p, part]
                    above[at, there] = other[z * line + p, part]

        def stored(name, slot, size):
            first = own_rows[name] + slot * size
            return store[first : first + size]

        for s in range(slots):
            vectors = jnp.concatenate([above[rows[s, k]] for k in range(touched)], 1)
            correction = dot(vectors, stored("panels", s, touched * width))
            shifted = stored("solved", s, width).astype(F32) - correction
            live = jnp.where(s < count[0, 0], 1.0, 0.0)
            result = dot(shifted.astype(BF16), stored("inverse", s, width)) * live
            sample[s] = result.T.astype(BF16)
        own = core * line + lax.axis_index("panel")
        sample1[...] = above[own].astype(F32).T.astype(BF16)
        own = own + (lax.axis_index("pair") + 1) * split
        sample2[...] = above[own].astype(F32).T.astype(BF16)

    block = whole.shape[1:]
    return pl.pallas_call(
        kernel,
        out_shape=(
            jax.ShapeDtypeStruct((slots,) + block, BF16),
            jax.ShapeDtypeStruct(block, BF16),
            jax.ShapeDtypeStruct(block, BF16),
        ),
        in_specs=[SMEM, SMEM] + [VMEM] * 4,
        out_specs=(VMEM,) * 3,
        scratch_shapes=[pltpu.VMEM((split + 2 * mine.shape[0],) + block, BF16)],
        compiler_params=PARAMS,
        name="leaf_backward",
    )(rows, count, whole, mine, other, store)


def exchange(blocks, axes):
    return lax.all_to_all(blocks, axes, 0, 0, tiled=True)


def swapped(array):
    return lax.ppermute(array, "core", [(0, 1), (1, 0)])


def body(
    leaf_rhs,
    leaf_inverse,
    leaf_panel,
    panel_rows,
    live_count,
    sep1_rhs,
    sep1_inverse,
    sep1_panel,
    sep2_rhs,
    sep2_inverse,
):
    rhs, inverse, panels = leaf_rhs[0, 0], leaf_inverse[0, 0], leaf_panel[0, 0]
    rows = panel_rows[0, 0]
    inverse1, inverse2, panel1 = sep1_inverse[0, 0], sep2_inverse[0, 0], sep1_panel[0, 0]
    width = inverse.shape[1]
    first_blocks = inverse1.shape[0] // width
    second_blocks = inverse2.shape[0] // width
    rows1, rows2 = inverse1.shape[0], inverse2.shape[0]
    places = store_rows(rows1, rows2, rows.shape[0], rows.shape[1], width)
    panel1_at, inverse2_at = places[0]["panel1"], places[0]["inverse2"]
    terms_at = places[0]["terms"]

    send1, store, keep = leaf_forward(
        places,
        live_count,
        rows,
        rhs,
        inverse,
        panels,
        sep1_rhs[0, 0],
        sep2_rhs[0, 0],
        inverse1,
        panel1,
        inverse2,
    )
    other = swapped(store)
    partial1 = side_partials(exchange(send1, FIRST), store, other, 0, rows1)
    raised, solved1_t = raise_terms(
        exchange(partial1, LINE), keep, store, other, panel1_at, rows2, terms_at
    )
    partial2 = side_partials(exchange(raised, CHIPS), store, other, inverse2_at, rows2)
    whole_solved = exchange(turned_sum(exchange(partial2, CHIPS)), CHIPS)

    whole_second = exchange(
        back_step(whole_solved, store, other, inverse2_at, second_blocks // 2), CHIPS
    )
    shifted = back_step(whole_second, store, other, panel1_at, first_blocks // 2, solved1_t)
    whole_shifted = exchange(shifted, LINE)
    other_second = swapped(lax.optimization_barrier((whole_second, shifted))[0])
    whole_shifted, other_second = lax.optimization_barrier((whole_shifted, other_second))
    whole_first = exchange(back_step(whole_shifted, store, other, 0, first_blocks), FIRST)
    leaf_sample, sample1, sample2 = leaf_backward(
        places, rows, live_count, whole_first, whole_second, other_second, store
    )
    return (leaf_sample[None, None], sample1[None, None], sample2[None, None])


def solution(mesh):
    places = mesh.devices.reshape(-1, 2, 2, mesh.shape["panel"])
    fine = Mesh(places, ("group", "pair", "core", "panel"))
    leaf = ("group", "pair", "core")

    def spec(rank):
        return P("panel", leaf, *(None,) * (rank - 2))

    return jax.shard_map(
        body,
        mesh=fine,
        in_specs=tuple(spec(rank) for rank in (5, 5, 6, 4, 2, 4, 4, 4, 4, 4)),
        out_specs=tuple(spec(rank) for rank in (5, 4, 4)),
        check_vma=False,
    )
```

```python
import jax
import jax.numpy as jnp
from jax import lax
from jax.experimental import pallas as pl
from jax.experimental.pallas import tpu as pltpu
from jax.sharding import Mesh, PartitionSpec as P

FIRST = ("core", "panel")
CHIPS = ("pair", "panel")
LINE = ("panel",)
F32, BF16 = jnp.float32, jnp.bfloat16
VMEM = pl.BlockSpec(memory_space=pltpu.VMEM)
SMEM = pl.BlockSpec(memory_space=pltpu.SMEM)
HBM = pl.BlockSpec(memory_space=pltpu.HBM)
PARAMS = pltpu.CompilerParams(vmem_limit_bytes=24 << 20)


def in_hbm(*arrays):
    return [pltpu.with_memory_space_constraint(array, pltpu.HBM) for array in arrays]


def dot(left, right):
    return lax.dot_general(left, right, (((1,), (0,)), ((), ())), preferred_element_type=F32)


def half_lanes(block):
    return lax.broadcasted_iota(jnp.int32, block.shape, 1) < block.shape[1] // 2


def turned(block):
    return pltpu.roll(block, block.shape[1] // 2, 1)


def packed(lower, upper):
    low = half_lanes(lower)
    return jnp.where(low, lower, turned(upper)), jnp.where(low, turned(lower), upper)


def start_loads(sems, *pairs):
    loads = [pltpu.make_async_copy(*pair, sems.at[i]) for i, pair in enumerate(pairs)]
    for load in loads:
        load.start()
    return loads


def store_rows(rows1, rows2, slots, touched, width):
    sizes = {
        "inverse1": rows1,
        "panel1": rows2,
        "inverse2": rows2,
        "terms": rows2 // 2,
        "panels": slots * touched * width,
        "inverse": slots * width,
        "solved": slots * width,
    }
    places, end = {}, 0
    for name, size in sizes.items():
        places[name] = end
        end += size
    return places, end


def leaf_forward(
    places, count, rows, rhs, inverse, panels, side1, side2, inverse1, panel1, inverse2
):
    block = rhs.shape[1:]
    width = block[0]
    slots, touched = rows.shape
    first_blocks, second_blocks = inverse1.shape[0] // width, inverse2.shape[0] // width
    halves, line = second_blocks // 2, first_blocks // 2
    own_rows, all_rows = places

    def kernel(
        rows_h,
        count,
        rhs,
        inverse,
        panels,
        side1,
        side2,
        inverse1,
        panel1,
        inverse2,
        send,
        store,
        keep,
        total,
        rows,
        rhs_v,
        side1_v,
        side2_v,
        sems,
        more_sems,
    ):
        def part(name, start=0, size=None, of=None):
            first = own_rows[name] + start
            return slice(first, first + (of.shape[0] if size is None else size))

        loads = start_loads(
            sems,
            (inverse, store.at[part("inverse", of=inverse)]),
            (rhs, rhs_v),
            (panels, store.at[part("panels", of=panels)]),
            (rows_h, rows),
            (side1, side1_v),
            (side2, side2_v),
        )
        matrices = start_loads(
            more_sems,
            (inverse1, store.at[part("inverse1", of=inverse1)]),
            (panel1, store.at[part("panel1", of=panel1)]),
            (inverse2, store.at[part("inverse2", of=inverse2)]),
        )
        core = lax.axis_index("core")
        total[...] = jnp.zeros_like(total)
        loads[0].wait()
        loads[1].wait()
        solved = []
        for s in range(slots):
            live = jnp.where(s < count[0, 0], 1.0, 0.0)
            piece = dot(store[part("inverse", s * width, width)], rhs_v[s]) * live
            piece = piece.astype(BF16)
            store[part("solved", s * width, width)] = piece.astype(F32).T.astype(BF16)
            solved.append(piece)
        loads[2].wait()
        loads[3].wait()
        for s in range(slots):
            tall = touched * width
            products = dot(store[part("panels", s * tall, tall)], solved[s])
            for k in range(touched):
                total[rows[s, k]] += products[k * width : (k + 1) * width]
        loads[4].wait()
        loads[5].wait()
        own = core * line + lax.axis_index("panel")
        total[own] -= side1_v[...].astype(F32)
        own = own + (lax.axis_index("pair") + 1) * first_blocks
        total[own] -= side2_v[...].astype(F32)
        for p in range(line):
            zero, one = packed(total[p], total[line + p])
            send[p] = zero.astype(BF16)
            send[line + p] = one.astype(BF16)
        for z in range(2):
            for p in range(line):
                at = (z + 1) * first_blocks + p
                zero, one = packed(total[at], total[at + line])
                at = z * line + p
                keep[at] = jnp.where(core == 0, zero, one)
                away = jnp.where(core == 0, one, zero)
                store[part("terms", at * width, width)] = away.astype(BF16)
        for load in matrices:
            load.wait()

    arrays = in_hbm(
        rhs,
        inverse.reshape(-1, width),
        panels.reshape(-1, width),
        side1,
        side2,
        inverse1,
        panel1,
        inverse2,
    )
    return pl.pallas_call(
        kernel,
        out_shape=(
            jax.ShapeDtypeStruct((first_blocks,) + block, BF16),
            jax.ShapeDtypeStruct((all_rows, width), BF16),
            jax.ShapeDtypeStruct((halves,) + block, F32),
        ),
        in_specs=[HBM, SMEM] + [HBM] * len(arrays),
        out_specs=(VMEM,) * 3,
        scratch_shapes=[
            pltpu.VMEM((first_blocks + second_blocks,) + block, F32),
            pltpu.SMEM(rows.shape, rows.dtype),
            pltpu.VMEM(rhs.shape, BF16),
            pltpu.VMEM(side1.shape, BF16),
            pltpu.VMEM(side2.shape, BF16),
            pltpu.SemaphoreType.DMA((6,)),
            pltpu.SemaphoreType.DMA((3,)),
        ],
        compiler_params=PARAMS,
        name="leaf_forward",
    )(*in_hbm(rows), count, *arrays)


def column_products(piece, mine, other, first_row, row_count):
    low = half_lanes(piece)
    across = turned(piece)
    zero = jnp.zeros_like(piece)
    lower = (jnp.where(low, piece, zero), jnp.where(low, across, zero))
    upper = (jnp.where(low, zero, across), jnp.where(low, zero, piece))
    swap = lax.axis_index("core") == 1

    def ordered(two):
        return [jnp.where(swap, two[1], two[0]), jnp.where(swap, two[0], two[1])]

    weights = jnp.concatenate(ordered(lower) + ordered(upper), 0).astype(BF16)
    half = mine.shape[1] * 4
    parts = []
    for start in range(first_row, first_row + row_count, 2 * half):
        middle = start + half
        wide = jnp.concatenate(
            [
                mine[start:middle],
                other[start:middle],
                mine[middle : middle + half],
                other[middle : middle + half],
            ],
            1,
        )
        parts.append(dot(wide, weights))
    return parts


def side_partials(received, mine, other, first_row, row_count):
    width = mine.shape[1]

    def kernel(received, mine, other, partials):
        side = -received[...].astype(F32).sum(axis=0)
        side = side.astype(BF16).astype(F32)
        for z, part in enumerate(column_products(side, mine, other, first_row, row_count)):
            for p in range(4):
                partials[z * 4 + p] = part[p * width : (p + 1) * width].astype(BF16)

    return pl.pallas_call(
        kernel,
        out_shape=jax.ShapeDtypeStruct((row_count // width // 2,) + received.shape[1:], BF16),
        in_specs=[VMEM] * 3,
        out_specs=VMEM,
        compiler_params=PARAMS,
        name="side_partials",
    )(received, mine, other)


def raise_terms(received, keep, mine, other, first_row, row_count, terms_row):
    width = mine.shape[1]

    def kernel(received, keep, mine, other, raised, solved_t):
        piece = received[...].astype(F32).sum(axis=0)
        piece = piece.astype(BF16).astype(F32)
        for z, part in enumerate(column_products(piece, mine, other, first_row, row_count)):
            for p in range(4):
                at = z * 4 + p
                came = other[terms_row + at * width : terms_row + (at + 1) * width]
                terms = keep[at] + came.astype(F32)
                raised[at] = (part[p * width : (p + 1) * width] + terms).astype(BF16)
        solved_t[...] = piece.T.astype(BF16)

    return pl.pallas_call(
        kernel,
        out_shape=(
            jax.ShapeDtypeStruct(keep.shape, BF16),
            jax.ShapeDtypeStruct(received.shape[1:], BF16),
        ),
        in_specs=[VMEM] * 4,
        out_specs=(VMEM,) * 2,
        compiler_params=PARAMS,
        name="raise_terms",
    )(received, keep, mine, other)


def turn_kernel(received, copies):
    piece = received[...].astype(F32).sum(axis=0).T.astype(BF16)
    for i in range(copies.shape[0]):
        copies[i] = piece


def turned_sum(received):
    return pl.pallas_call(
        turn_kernel,
        out_shape=jax.ShapeDtypeStruct(received.shape, BF16),
        in_specs=[VMEM],
        out_specs=VMEM,
        compiler_params=PARAMS,
        name="turned_sum",
    )(received)


def back_step(whole, mine, other, first_row, targets, base=None):
    panels = 4
    half = whole.shape[1] // 2
    rows = pl.ds(first_row, 2 * whole.shape[0] * mine.shape[1])

    def kernel(whole, mine, other, *rest):
        pieces = []
        for z in range(whole.shape[0] // panels):
            for c in range(2):
                for p in range(panels):
                    pieces.append(whole[z * panels + p, c * half : (c + 1) * half])
        vectors = jnp.concatenate(pieces, 1)
        mine_t = dot(vectors, mine[rows])
        other_t = dot(vectors, other[rows])
        swap = lax.axis_index("core") == 1
        result = jnp.concatenate(
            [jnp.where(swap, other_t, mine_t), jnp.where(swap, mine_t, other_t)], 0
        )
        if base is not None:
            result = rest[0][...].astype(F32) - result
        copies = rest[-1]
        result = result.astype(BF16)
        for i in range(targets):
            copies[i] = result

    operands = (whole, mine, other) + (() if base is None else (base,))
    return pl.pallas_call(
        kernel,
        out_shape=jax.ShapeDtypeStruct((targets,) + whole.shape[1:], BF16),
        in_specs=[VMEM] * len(operands),
        out_specs=VMEM,
        compiler_params=PARAMS,
        name="back_step",
    )(*operands)


def full_step(whole, pieces, second):
    line, width = whole.shape[:2]
    half = width // 2
    height = 2 * line * width

    def piece_rows(piece):
        return slice(piece * height, (piece + 1) * height)

    def kernel(whole, pieces, second, joined, pieces_v, sems):
        loads = start_loads(
            sems, *((pieces.at[at], pieces_v.at[at]) for at in map(piece_rows, range(2 * line)))
        )
        vectors = jnp.concatenate(
            [whole[p, c * half : (c + 1) * half] for c in range(2) for p in range(line)], 1
        )
        joined[line:] = second[...]
        for c in range(2):
            for p in range(line):
                loads[c * line + p].wait()
                result = dot(vectors, pieces_v[piece_rows(c * line + p)])
                joined[p, c * half : (c + 1) * half] = result.astype(BF16)

    return pl.pallas_call(
        kernel,
        out_shape=jax.ShapeDtypeStruct((line + second.shape[0],) + whole.shape[1:], BF16),
        in_specs=[VMEM, HBM, VMEM],
        out_specs=VMEM,
        scratch_shapes=[pltpu.VMEM(pieces.shape, BF16), pltpu.SemaphoreType.DMA((2 * line,))],
        compiler_params=PARAMS,
        name="full_step",
    )(whole, *in_hbm(pieces), second)


def leaf_backward(places, rows, count, mine, other, store):
    slots, touched = rows.shape
    width = mine.shape[1]
    half = width // 2
    line = mine.shape[0] // 3
    own_rows, _ = places

    def kernel(rows, count, mine, other, store, sample, sample1, sample2, above):
        core = lax.axis_index("core")
        here = pl.ds(pl.multiple_of(core * half, half), half)
        there = pl.ds(pl.multiple_of((1 - core) * half, half), half)
        for z in range(3):
            for c in range(2):
                part = slice(c * half, (c + 1) * half)
                for p in range(line):
                    at = (2 * z + c) * line + p
                    above[at, here] = mine[z * line + p, part]
                    above[at, there] = other[z * line + p, part]

        def stored(name, slot, size):
            first = own_rows[name] + slot * size
            return store[first : first + size]

        for s in range(slots):
            vectors = jnp.concatenate([above[rows[s, k]] for k in range(touched)], 1)
            correction = dot(vectors, stored("panels", s, touched * width))
            shifted = stored("solved", s, width).astype(F32) - correction
            live = jnp.where(s < count[0, 0], 1.0, 0.0)
            result = dot(shifted.astype(BF16), stored("inverse", s, width)) * live
            sample[s] = result.T.astype(BF16)
        own = core * line + lax.axis_index("panel")
        sample1[...] = above[own].astype(F32).T.astype(BF16)
        own = own + (lax.axis_index("pair") + 1) * 2 * line
        sample2[...] = above[own].astype(F32).T.astype(BF16)

    block = mine.shape[1:]
    return pl.pallas_call(
        kernel,
        out_shape=(
            jax.ShapeDtypeStruct((slots,) + block, BF16),
            jax.ShapeDtypeStruct(block, BF16),
            jax.ShapeDtypeStruct(block, BF16),
        ),
        in_specs=[SMEM, SMEM] + [VMEM] * 3,
        out_specs=(VMEM,) * 3,
        scratch_shapes=[pltpu.VMEM((2 * mine.shape[0],) + block, BF16)],
        compiler_params=PARAMS,
        name="leaf_backward",
    )(rows, count, mine, other, store)


def exchange(blocks, axes):
    return lax.all_to_all(blocks, axes, 0, 0, tiled=True)


def swapped(array):
    return lax.ppermute(array, "core", [(0, 1), (1, 0)])


def body(
    leaf_rhs,
    leaf_inverse,
    leaf_panel,
    panel_rows,
    live_count,
    sep1_rhs,
    sep1_inverse,
    sep1_panel,
    sep2_rhs,
    sep2_inverse,
):
    rhs, inverse, panels = leaf_rhs[0, 0], leaf_inverse[0, 0], leaf_panel[0, 0]
    rows = panel_rows[0, 0]
    inverse1, inverse2, panel1 = sep1_inverse[0, 0], sep2_inverse[0, 0], sep1_panel[0, 0]
    width = inverse.shape[1]
    first_blocks = inverse1.shape[0] // width
    second_blocks = inverse2.shape[0] // width
    rows1, rows2 = inverse1.shape[0], inverse2.shape[0]
    places = store_rows(rows1, rows2, rows.shape[0], rows.shape[1], width)
    panel1_at, inverse2_at = places[0]["panel1"], places[0]["inverse2"]
    terms_at = places[0]["terms"]

    pieces = lax.all_gather(inverse1, FIRST, axis=0, tiled=True)
    send1, store, keep = leaf_forward(
        places,
        live_count,
        rows,
        rhs,
        inverse,
        panels,
        sep1_rhs[0, 0],
        sep2_rhs[0, 0],
        inverse1,
        panel1,
        inverse2,
    )
    other = swapped(store)
    partial1 = side_partials(exchange(send1, FIRST), store, other, 0, rows1)
    raised, solved1_t = raise_terms(
        exchange(partial1, LINE), keep, store, other, panel1_at, rows2, terms_at
    )
    partial2 = side_partials(exchange(raised, CHIPS), store, other, inverse2_at, rows2)
    whole_solved = exchange(turned_sum(exchange(partial2, CHIPS)), CHIPS)

    whole_second = exchange(
        back_step(whole_solved, store, other, inverse2_at, second_blocks // 2), CHIPS
    )
    shifted = back_step(whole_second, store, other, panel1_at, first_blocks // 2, solved1_t)
    whole_shifted = exchange(shifted, LINE)
    joined = full_step(whole_shifted, pieces, whole_second)
    leaf_sample, sample1, sample2 = leaf_backward(
        places, rows, live_count, joined, swapped(joined), store
    )
    return (leaf_sample[None, None], sample1[None, None], sample2[None, None])


def solution(mesh):
    places = mesh.devices.reshape(-1, 2, 2, mesh.shape["panel"])
    fine = Mesh(places, ("group", "pair", "core", "panel"))
    leaf = ("group", "pair", "core")

    def spec(rank):
        return P("panel", leaf, *(None,) * (rank - 2))

    return jax.shard_map(
        body,
        mesh=fine,
        in_specs=tuple(spec(rank) for rank in (5, 5, 6, 4, 2, 4, 4, 4, 4, 4)),
        out_specs=tuple(spec(rank) for rank in (5, 4, 4)),
        check_vma=False,
    )
```

```python
import jax
import jax.numpy as jnp
from jax import lax
from jax.experimental import pallas as pl
from jax.experimental.pallas import tpu as pltpu
from jax.sharding import Mesh, PartitionSpec as P

FIRST = ("core", "panel")
CHIPS = ("pair", "panel")
LINE = ("panel",)
F32, BF16 = jnp.float32, jnp.bfloat16
VMEM = pl.BlockSpec(memory_space=pltpu.VMEM)
SMEM = pl.BlockSpec(memory_space=pltpu.SMEM)
HBM = pl.BlockSpec(memory_space=pltpu.HBM)
PARAMS = pltpu.CompilerParams(vmem_limit_bytes=24 << 20)


def in_hbm(*arrays):
    return [pltpu.with_memory_space_constraint(array, pltpu.HBM) for array in arrays]


def dot(left, right):
    return lax.dot_general(left, right, (((1,), (0,)), ((), ())), preferred_element_type=F32)


def half_lanes(block):
    return lax.broadcasted_iota(jnp.int32, block.shape, 1) < block.shape[1] // 2


def turned(block):
    return pltpu.roll(block, block.shape[1] // 2, 1)


def packed(lower, upper):
    low = half_lanes(lower)
    return jnp.where(low, lower, turned(upper)), jnp.where(low, turned(lower), upper)


def start_loads(sems, *pairs):
    loads = [pltpu.make_async_copy(*pair, sems.at[i]) for i, pair in enumerate(pairs)]
    for load in loads:
        load.start()
    return loads


def store_rows(rows1, rows2, slots, touched, width):
    sizes = {
        "inverse1": rows1,
        "panel1": rows2,
        "inverse2": rows2,
        "terms": rows2 // 2,
        "panels": slots * touched * width,
        "inverse": slots * width,
        "solved": slots * width,
    }
    places, end = {}, 0
    for name, size in sizes.items():
        places[name] = end
        end += size
    return places, end


def leaf_forward(
    places, count, rows, rhs, inverse, panels, side1, side2, inverse1, panel1, inverse2
):
    block = rhs.shape[1:]
    width = block[0]
    slots, touched = rows.shape
    first_blocks, second_blocks = inverse1.shape[0] // width, inverse2.shape[0] // width
    halves, line = second_blocks // 2, first_blocks // 2
    own_rows, all_rows = places

    def kernel(
        rows_h,
        count,
        rhs,
        inverse,
        panels,
        side1,
        side2,
        inverse1,
        panel1,
        inverse2,
        send,
        store,
        keep,
        total,
        rows,
        rhs_v,
        side1_v,
        side2_v,
        sems,
        more_sems,
    ):
        def part(name, start=0, size=None, of=None):
            first = own_rows[name] + start
            return slice(first, first + (of.shape[0] if size is None else size))

        loads = start_loads(
            sems,
            (inverse, store.at[part("inverse", of=inverse)]),
            (rhs, rhs_v),
            (panels, store.at[part("panels", of=panels)]),
            (rows_h, rows),
            (side1, side1_v),
            (side2, side2_v),
        )
        matrices = start_loads(
            more_sems,
            (inverse1, store.at[part("inverse1", of=inverse1)]),
            (panel1, store.at[part("panel1", of=panel1)]),
            (inverse2, store.at[part("inverse2", of=inverse2)]),
        )
        core = lax.axis_index("core")
        total[...] = jnp.zeros_like(total)
        loads[0].wait()
        loads[1].wait()
        solved = []
        for s in range(slots):
            live = jnp.where(s < count[0, 0], 1.0, 0.0)
            piece = dot(store[part("inverse", s * width, width)], rhs_v[s]) * live
            piece = piece.astype(BF16)
            store[part("solved", s * width, width)] = piece.astype(F32).T.astype(BF16)
            solved.append(piece)
        loads[2].wait()
        loads[3].wait()
        for s in range(slots):
            tall = touched * width
            products = dot(store[part("panels", s * tall, tall)], solved[s])
            for k in range(touched):
                total[rows[s, k]] += products[k * width : (k + 1) * width]
        loads[4].wait()
        loads[5].wait()
        own = core * line + lax.axis_index("panel")
        total[own] -= side1_v[...].astype(F32)
        own = own + (lax.axis_index("pair") + 1) * first_blocks
        total[own] -= side2_v[...].astype(F32)
        for p in range(line):
            zero, one = packed(total[p], total[line + p])
            send[p] = zero.astype(BF16)
            send[line + p] = one.astype(BF16)
        for z in range(2):
            for p in range(line):
                at = (z + 1) * first_blocks + p
                zero, one = packed(total[at], total[at + line])
                at = z * line + p
                keep[at] = jnp.where(core == 0, zero, one)
                away = jnp.where(core == 0, one, zero)
                store[part("terms", at * width, width)] = away.astype(BF16)
        for load in matrices:
            load.wait()

    arrays = in_hbm(
        rhs,
        inverse.reshape(-1, width),
        panels.reshape(-1, width),
        side1,
        side2,
        inverse1,
        panel1,
        inverse2,
    )
    return pl.pallas_call(
        kernel,
        out_shape=(
            jax.ShapeDtypeStruct((first_blocks,) + block, BF16),
            jax.ShapeDtypeStruct((all_rows, width), BF16),
            jax.ShapeDtypeStruct((halves,) + block, F32),
        ),
        in_specs=[HBM, SMEM] + [HBM] * len(arrays),
        out_specs=(VMEM,) * 3,
        scratch_shapes=[
            pltpu.VMEM((first_blocks + second_blocks,) + block, F32),
            pltpu.SMEM(rows.shape, rows.dtype),
            pltpu.VMEM(rhs.shape, BF16),
            pltpu.VMEM(side1.shape, BF16),
            pltpu.VMEM(side2.shape, BF16),
            pltpu.SemaphoreType.DMA((6,)),
            pltpu.SemaphoreType.DMA((3,)),
        ],
        compiler_params=PARAMS,
        name="leaf_forward",
    )(*in_hbm(rows), count, *arrays)


def column_products(piece, mine, other, first_row, row_count):
    low = half_lanes(piece)
    across = turned(piece)
    zero = jnp.zeros_like(piece)
    lower = (jnp.where(low, piece, zero), jnp.where(low, across, zero))
    upper = (jnp.where(low, zero, across), jnp.where(low, zero, piece))
    swap = lax.axis_index("core") == 1

    def ordered(two):
        return [jnp.where(swap, two[1], two[0]), jnp.where(swap, two[0], two[1])]

    weights = jnp.concatenate(ordered(lower) + ordered(upper), 0).astype(BF16)
    half = mine.shape[1] * 4
    parts = []
    for start in range(first_row, first_row + row_count, 2 * half):
        middle = start + half
        wide = jnp.concatenate(
            [
                mine[start:middle],
                other[start:middle],
                mine[middle : middle + half],
                other[middle : middle + half],
            ],
            1,
        )
        parts.append(dot(wide, weights))
    return parts


def side_partials(received, mine, other, first_row, row_count):
    width = mine.shape[1]

    def kernel(received, mine, other, partials):
        side = -received[...].astype(F32).sum(axis=0)
        side = side.astype(BF16).astype(F32)
        for z, part in enumerate(column_products(side, mine, other, first_row, row_count)):
            for p in range(4):
                partials[z * 4 + p] = part[p * width : (p + 1) * width].astype(BF16)

    return pl.pallas_call(
        kernel,
        out_shape=jax.ShapeDtypeStruct((row_count // width // 2,) + received.shape[1:], BF16),
        in_specs=[VMEM] * 3,
        out_specs=VMEM,
        compiler_params=PARAMS,
        name="side_partials",
    )(received, mine, other)


def raise_terms(received, keep, mine, other, first_row, row_count, terms_row):
    width = mine.shape[1]

    def kernel(received, keep, mine, other, raised, solved_t):
        piece = received[...].astype(F32).sum(axis=0)
        piece = piece.astype(BF16).astype(F32)
        for z, part in enumerate(column_products(piece, mine, other, first_row, row_count)):
            for p in range(4):
                at = z * 4 + p
                came = other[terms_row + at * width : terms_row + (at + 1) * width]
                terms = keep[at] + came.astype(F32)
                raised[at] = (part[p * width : (p + 1) * width] + terms).astype(BF16)
        solved_t[...] = piece.T.astype(BF16)

    return pl.pallas_call(
        kernel,
        out_shape=(
            jax.ShapeDtypeStruct(keep.shape, BF16),
            jax.ShapeDtypeStruct(received.shape[1:], BF16),
        ),
        in_specs=[VMEM] * 4,
        out_specs=(VMEM,) * 2,
        compiler_params=PARAMS,
        name="raise_terms",
    )(received, keep, mine, other)


def turn_kernel(received, copies):
    piece = received[...].astype(F32).sum(axis=0).T.astype(BF16)
    for i in range(copies.shape[0]):
        copies[i] = piece


def turned_sum(received):
    return pl.pallas_call(
        turn_kernel,
        out_shape=jax.ShapeDtypeStruct(received.shape, BF16),
        in_specs=[VMEM],
        out_specs=VMEM,
        compiler_params=PARAMS,
        name="turned_sum",
    )(received)


def back_step(whole, mine, other, first_row, targets, base=None):
    panels = 4
    half = whole.shape[1] // 2
    rows = pl.ds(first_row, 2 * whole.shape[0] * mine.shape[1])

    def kernel(whole, mine, other, *rest):
        pieces = []
        for z in range(whole.shape[0] // panels):
            for c in range(2):
                for p in range(panels):
                    pieces.append(whole[z * panels + p, c * half : (c + 1) * half])
        vectors = jnp.concatenate(pieces, 1)
        mine_t = dot(vectors, mine[rows])
        other_t = dot(vectors, other[rows])
        swap = lax.axis_index("core") == 1
        result = jnp.concatenate(
            [jnp.where(swap, other_t, mine_t), jnp.where(swap, mine_t, other_t)], 0
        )
        if base is not None:
            result = rest[0][...].astype(F32) - result
        copies = rest[-1]
        result = result.astype(BF16)
        for i in range(targets):
            copies[i] = result

    operands = (whole, mine, other) + (() if base is None else (base,))
    return pl.pallas_call(
        kernel,
        out_shape=jax.ShapeDtypeStruct((targets,) + whole.shape[1:], BF16),
        in_specs=[VMEM] * len(operands),
        out_specs=VMEM,
        compiler_params=PARAMS,
        name="back_step",
    )(*operands)


def leaf_backward(places, rows, count, whole, mine, other, store):
    slots, touched = rows.shape
    width = whole.shape[1]
    half = width // 2
    split = whole.shape[0]
    line = split // 2
    own_rows, _ = places

    def kernel(rows, count, whole, mine, other, store, sample, sample1, sample2, above):
        core = lax.axis_index("core")
        here = pl.ds(pl.multiple_of(core * half, half), half)
        there = pl.ds(pl.multiple_of((1 - core) * half, half), half)
        for c in range(2):
            part = slice(c * half, (c + 1) * half)
            for p in range(line):
                for h in range(2):
                    above[c * line + p, h * half : (h + 1) * half] = whole[h * line + p, part]
                for z in range(2):
                    at = (z + 1) * split + c * line + p
                    above[at, here] = mine[z * line + p, part]
                    above[at, there] = other[z * line + p, part]

        def stored(name, slot, size):
            first = own_rows[name] + slot * size
            return store[first : first + size]

        for s in range(slots):
            vectors = jnp.concatenate([above[rows[s, k]] for k in range(touched)], 1)
            correction = dot(vectors, stored("panels", s, touched * width))
            shifted = stored("solved", s, width).astype(F32) - correction
            live = jnp.where(s < count[0, 0], 1.0, 0.0)
            result = dot(shifted.astype(BF16), stored("inverse", s, width)) * live
            sample[s] = result.T.astype(BF16)
        own = core * line + lax.axis_index("panel")
        sample1[...] = above[own].astype(F32).T.astype(BF16)
        own = own + (lax.axis_index("pair") + 1) * split
        sample2[...] = above[own].astype(F32).T.astype(BF16)

    block = whole.shape[1:]
    return pl.pallas_call(
        kernel,
        out_shape=(
            jax.ShapeDtypeStruct((slots,) + block, BF16),
            jax.ShapeDtypeStruct(block, BF16),
            jax.ShapeDtypeStruct(block, BF16),
        ),
        in_specs=[SMEM, SMEM] + [VMEM] * 4,
        out_specs=(VMEM,) * 3,
        scratch_shapes=[pltpu.VMEM((split + 2 * mine.shape[0],) + block, BF16)],
        compiler_params=PARAMS,
        name="leaf_backward",
    )(rows, count, whole, mine, other, store)


def exchange(blocks, axes):
    return lax.all_to_all(blocks, axes, 0, 0, tiled=True)


def swapped(array):
    return lax.ppermute(array, "core", [(0, 1), (1, 0)])


def body(
    leaf_rhs,
    leaf_inverse,
    leaf_panel,
    panel_rows,
    live_count,
    sep1_rhs,
    sep1_inverse,
    sep1_panel,
    sep2_rhs,
    sep2_inverse,
):
    rhs, inverse, panels = leaf_rhs[0, 0], leaf_inverse[0, 0], leaf_panel[0, 0]
    rows = panel_rows[0, 0]
    inverse1, inverse2, panel1 = sep1_inverse[0, 0], sep2_inverse[0, 0], sep1_panel[0, 0]
    width = inverse.shape[1]
    first_blocks = inverse1.shape[0] // width
    second_blocks = inverse2.shape[0] // width
    rows1, rows2 = inverse1.shape[0], inverse2.shape[0]
    places = store_rows(rows1, rows2, rows.shape[0], rows.shape[1], width)
    panel1_at, inverse2_at = places[0]["panel1"], places[0]["inverse2"]
    terms_at = places[0]["terms"]

    send1, store, keep = leaf_forward(
        places,
        live_count,
        rows,
        rhs,
        inverse,
        panels,
        sep1_rhs[0, 0],
        sep2_rhs[0, 0],
        inverse1,
        panel1,
        inverse2,
    )
    other = swapped(store)
    summed1 = exchange(send1, FIRST).astype(F32).sum(axis=0, keepdims=True)
    partial1 = side_partials(summed1, store, other, 0, rows1)
    raised, solved1_t = raise_terms(
        exchange(partial1, LINE), keep, store, other, panel1_at, rows2, terms_at
    )
    partial2 = side_partials(exchange(raised, CHIPS), store, other, inverse2_at, rows2)
    whole_solved = exchange(turned_sum(exchange(partial2, CHIPS)), CHIPS)

    whole_second = exchange(
        back_step(whole_solved, store, other, inverse2_at, second_blocks // 2), CHIPS
    )
    shifted = back_step(whole_second, store, other, panel1_at, first_blocks // 2, solved1_t)
    whole_shifted = exchange(shifted, LINE)
    other_second = swapped(lax.optimization_barrier((whole_second, shifted))[0])
    sample1_t, other_second = lax.optimization_barrier(
        (back_step(whole_shifted, store, other, 0, first_blocks), other_second)
    )
    whole_first = exchange(sample1_t, FIRST)
    leaf_sample, sample1, sample2 = leaf_backward(
        places, rows, live_count, whole_first, whole_second, other_second, store
    )
    return (leaf_sample[None, None], sample1[None, None], sample2[None, None])


def solution(mesh):
    places = mesh.devices.reshape(-1, 2, 2, mesh.shape["panel"])
    fine = Mesh(places, ("group", "pair", "core", "panel"))
    leaf = ("group", "pair", "core")

    def spec(rank):
        return P("panel", leaf, *(None,) * (rank - 2))

    return jax.shard_map(
        body,
        mesh=fine,
        in_specs=tuple(spec(rank) for rank in (5, 5, 6, 4, 2, 4, 4, 4, 4, 4)),
        out_specs=tuple(spec(rank) for rank in (5, 4, 4)),
        check_vma=False,
    )
```

```python
import jax
import jax.numpy as jnp
from jax import lax
from jax.experimental import pallas as pl
from jax.experimental.pallas import tpu as pltpu
from jax.sharding import Mesh, PartitionSpec as P

FIRST = ("core", "panel")
CHIPS = ("pair", "panel")
LINE = ("panel",)
F32, BF16 = jnp.float32, jnp.bfloat16
VMEM = pl.BlockSpec(memory_space=pltpu.VMEM)
SMEM = pl.BlockSpec(memory_space=pltpu.SMEM)
HBM = pl.BlockSpec(memory_space=pltpu.HBM)
PARAMS = pltpu.CompilerParams(vmem_limit_bytes=24 << 20)


def in_hbm(*arrays):
    return [pltpu.with_memory_space_constraint(array, pltpu.HBM) for array in arrays]


def dot(left, right):
    return lax.dot_general(left, right, (((1,), (0,)), ((), ())), preferred_element_type=F32)


def half_lanes(block):
    return lax.broadcasted_iota(jnp.int32, block.shape, 1) < block.shape[1] // 2


def turned(block):
    return pltpu.roll(block, block.shape[1] // 2, 1)


def packed(lower, upper):
    low = half_lanes(lower)
    return jnp.where(low, lower, turned(upper)), jnp.where(low, turned(lower), upper)


def start_loads(sems, *pairs):
    loads = [pltpu.make_async_copy(*pair, sems.at[i]) for i, pair in enumerate(pairs)]
    for load in loads:
        load.start()
    return loads


def store_rows(rows1, rows2, slots, touched, width):
    sizes = {
        "inverse1": rows1,
        "panel1": rows2,
        "inverse2": rows2,
        "terms": rows2 // 2,
        "panels": slots * touched * width,
        "inverse": slots * width,
        "solved": slots * width,
    }
    places, end = {}, 0
    for name, size in sizes.items():
        places[name] = end
        end += size
    return places, end


def leaf_forward(
    places, count, rows, rhs, inverse, panels, side1, side2, inverse1, panel1, inverse2
):
    block = rhs.shape[1:]
    width = block[0]
    slots, touched = rows.shape
    first_blocks, second_blocks = inverse1.shape[0] // width, inverse2.shape[0] // width
    halves, line = second_blocks // 2, first_blocks // 2
    own_rows, all_rows = places

    def kernel(
        rows_h,
        count,
        rhs,
        inverse,
        panels,
        side1,
        side2,
        inverse1,
        panel1,
        inverse2,
        send,
        store,
        keep,
        total,
        rows,
        rhs_v,
        side1_v,
        side2_v,
        sems,
        more_sems,
    ):
        def part(name, start=0, size=None, of=None):
            first = own_rows[name] + start
            return slice(first, first + (of.shape[0] if size is None else size))

        loads = start_loads(
            sems,
            (inverse, store.at[part("inverse", of=inverse)]),
            (rhs, rhs_v),
            (panels, store.at[part("panels", of=panels)]),
            (rows_h, rows),
            (side1, side1_v),
            (side2, side2_v),
        )
        matrices = start_loads(
            more_sems,
            (inverse1, store.at[part("inverse1", of=inverse1)]),
            (panel1, store.at[part("panel1", of=panel1)]),
            (inverse2, store.at[part("inverse2", of=inverse2)]),
        )
        core = lax.axis_index("core")
        total[...] = jnp.zeros_like(total)
        loads[0].wait()
        loads[1].wait()
        solved = []
        for s in range(slots):
            live = jnp.where(s < count[0, 0], 1.0, 0.0)
            piece = dot(store[part("inverse", s * width, width)], rhs_v[s]) * live
            piece = piece.astype(BF16)
            store[part("solved", s * width, width)] = piece.astype(F32).T.astype(BF16)
            solved.append(piece)
        loads[2].wait()
        loads[3].wait()
        for s in range(slots):
            tall = touched * width
            products = dot(store[part("panels", s * tall, tall)], solved[s])
            for k in range(touched):
                total[rows[s, k]] += products[k * width : (k + 1) * width]
        loads[4].wait()
        loads[5].wait()
        own = core * line + lax.axis_index("panel")
        total[own] -= side1_v[...].astype(F32)
        own = own + (lax.axis_index("pair") + 1) * first_blocks
        total[own] -= side2_v[...].astype(F32)
        send[...] = total[:first_blocks].astype(BF16)
        for z in range(2):
            for p in range(line):
                at = (z + 1) * first_blocks + p
                zero, one = packed(total[at], total[at + line])
                at = z * line + p
                keep[at] = jnp.where(core == 0, zero, one)
                away = jnp.where(core == 0, one, zero)
                store[part("terms", at * width, width)] = away.astype(BF16)
        for load in matrices:
            load.wait()

    arrays = in_hbm(
        rhs,
        inverse.reshape(-1, width),
        panels.reshape(-1, width),
        side1,
        side2,
        inverse1,
        panel1,
        inverse2,
    )
    return pl.pallas_call(
        kernel,
        out_shape=(
            jax.ShapeDtypeStruct((first_blocks,) + block, BF16),
            jax.ShapeDtypeStruct((all_rows, width), BF16),
            jax.ShapeDtypeStruct((halves,) + block, F32),
        ),
        in_specs=[HBM, SMEM] + [HBM] * len(arrays),
        out_specs=(VMEM,) * 3,
        scratch_shapes=[
            pltpu.VMEM((first_blocks + second_blocks,) + block, F32),
            pltpu.SMEM(rows.shape, rows.dtype),
            pltpu.VMEM(rhs.shape, BF16),
            pltpu.VMEM(side1.shape, BF16),
            pltpu.VMEM(side2.shape, BF16),
            pltpu.SemaphoreType.DMA((6,)),
            pltpu.SemaphoreType.DMA((3,)),
        ],
        compiler_params=PARAMS,
        name="leaf_forward",
    )(*in_hbm(rows), count, *arrays)


def column_products(piece, mine, other, first_row, row_count):
    low = half_lanes(piece)
    across = turned(piece)
    zero = jnp.zeros_like(piece)
    lower = (jnp.where(low, piece, zero), jnp.where(low, across, zero))
    upper = (jnp.where(low, zero, across), jnp.where(low, zero, piece))
    swap = lax.axis_index("core") == 1

    def ordered(two):
        return [jnp.where(swap, two[1], two[0]), jnp.where(swap, two[0], two[1])]

    weights = jnp.concatenate(ordered(lower) + ordered(upper), 0).astype(BF16)
    half = mine.shape[1] * 4
    parts = []
    for start in range(first_row, first_row + row_count, 2 * half):
        middle = start + half
        wide = jnp.concatenate(
            [
                mine[start:middle],
                other[start:middle],
                mine[middle : middle + half],
                other[middle : middle + half],
            ],
            1,
        )
        parts.append(dot(wide, weights))
    return parts


def first_partials(received, mine, row_count):
    width = mine.shape[1]
    line = received.shape[0] // 2

    def kernel(received, mine, partials):
        side = -received[...].astype(F32).sum(axis=0)
        product = dot(mine[:row_count], side.astype(BF16))
        for p in range(line):
            lower = product[p * width : (p + 1) * width]
            upper = product[(line + p) * width : (line + p + 1) * width]
            zero, one = packed(lower, upper)
            partials[p] = zero.astype(BF16)
            partials[line + p] = one.astype(BF16)

    return pl.pallas_call(
        kernel,
        out_shape=jax.ShapeDtypeStruct(received.shape, BF16),
        in_specs=[VMEM] * 2,
        out_specs=VMEM,
        compiler_params=PARAMS,
        name="first_partials",
    )(received, mine)


def side_partials(received, mine, other, first_row, row_count):
    width = mine.shape[1]

    def kernel(received, mine, other, partials):
        side = -received[...].astype(F32).sum(axis=0)
        side = side.astype(BF16).astype(F32)
        for z, part in enumerate(column_products(side, mine, other, first_row, row_count)):
            for p in range(4):
                partials[z * 4 + p] = part[p * width : (p + 1) * width].astype(BF16)

    return pl.pallas_call(
        kernel,
        out_shape=jax.ShapeDtypeStruct((row_count // width // 2,) + received.shape[1:], BF16),
        in_specs=[VMEM] * 3,
        out_specs=VMEM,
        compiler_params=PARAMS,
        name="side_partials",
    )(received, mine, other)


def raise_terms(received, keep, mine, other, first_row, row_count, terms_row):
    width = mine.shape[1]

    def kernel(received, keep, mine, other, raised, solved_t):
        piece = received[...].astype(F32).sum(axis=0)
        piece = piece.astype(BF16).astype(F32)
        for z, part in enumerate(column_products(piece, mine, other, first_row, row_count)):
            for p in range(4):
                at = z * 4 + p
                came = other[terms_row + at * width : terms_row + (at + 1) * width]
                terms = keep[at] + came.astype(F32)
                raised[at] = (part[p * width : (p + 1) * width] + terms).astype(BF16)
        solved_t[...] = piece.T.astype(BF16)

    return pl.pallas_call(
        kernel,
        out_shape=(
            jax.ShapeDtypeStruct(keep.shape, BF16),
            jax.ShapeDtypeStruct(received.shape[1:], BF16),
        ),
        in_specs=[VMEM] * 4,
        out_specs=(VMEM,) * 2,
        compiler_params=PARAMS,
        name="raise_terms",
    )(received, keep, mine, other)


def turn_kernel(received, copies):
    piece = received[...].astype(F32).sum(axis=0).T.astype(BF16)
    for i in range(copies.shape[0]):
        copies[i] = piece


def turned_sum(received):
    return pl.pallas_call(
        turn_kernel,
        out_shape=jax.ShapeDtypeStruct(received.shape, BF16),
        in_specs=[VMEM],
        out_specs=VMEM,
        compiler_params=PARAMS,
        name="turned_sum",
    )(received)


def back_step(whole, mine, other, first_row, targets, base=None):
    panels = 4
    half = whole.shape[1] // 2
    rows = pl.ds(first_row, 2 * whole.shape[0] * mine.shape[1])

    def kernel(whole, mine, other, *rest):
        pieces = []
        for z in range(whole.shape[0] // panels):
            for c in range(2):
                for p in range(panels):
                    pieces.append(whole[z * panels + p, c * half : (c + 1) * half])
        vectors = jnp.concatenate(pieces, 1)
        mine_t = dot(vectors, mine[rows])
        other_t = dot(vectors, other[rows])
        swap = lax.axis_index("core") == 1
        result = jnp.concatenate(
            [jnp.where(swap, other_t, mine_t), jnp.where(swap, mine_t, other_t)], 0
        )
        if base is not None:
            result = rest[0][...].astype(F32) - result
        copies = rest[-1]
        result = result.astype(BF16)
        for i in range(targets):
            copies[i] = result

    operands = (whole, mine, other) + (() if base is None else (base,))
    return pl.pallas_call(
        kernel,
        out_shape=jax.ShapeDtypeStruct((targets,) + whole.shape[1:], BF16),
        in_specs=[VMEM] * len(operands),
        out_specs=VMEM,
        compiler_params=PARAMS,
        name="back_step",
    )(*operands)


def leaf_backward(places, rows, count, whole, mine, other, store):
    slots, touched = rows.shape
    width = whole.shape[1]
    half = width // 2
    split = whole.shape[0]
    line = split // 2
    own_rows, _ = places

    def kernel(rows, count, whole, mine, other, store, sample, sample1, sample2, above):
        core = lax.axis_index("core")
        here = pl.ds(pl.multiple_of(core * half, half), half)
        there = pl.ds(pl.multiple_of((1 - core) * half, half), half)
        for c in range(2):
            part = slice(c * half, (c + 1) * half)
            for p in range(line):
                for h in range(2):
                    above[c * line + p, h * half : (h + 1) * half] = whole[h * line + p, part]
                for z in range(2):
                    at = (z + 1) * split + c * line + p
                    above[at, here] = mine[z * line + p, part]
                    above[at, there] = other[z * line + p, part]

        def stored(name, slot, size):
            first = own_rows[name] + slot * size
            return store[first : first + size]

        for s in range(slots):
            vectors = jnp.concatenate([above[rows[s, k]] for k in range(touched)], 1)
            correction = dot(vectors, stored("panels", s, touched * width))
            shifted = stored("solved", s, width).astype(F32) - correction
            live = jnp.where(s < count[0, 0], 1.0, 0.0)
            result = dot(shifted.astype(BF16), stored("inverse", s, width)) * live
            sample[s] = result.T.astype(BF16)
        own = core * line + lax.axis_index("panel")
        sample1[...] = above[own].astype(F32).T.astype(BF16)
        own = own + (lax.axis_index("pair") + 1) * split
        sample2[...] = above[own].astype(F32).T.astype(BF16)

    block = whole.shape[1:]
    return pl.pallas_call(
        kernel,
        out_shape=(
            jax.ShapeDtypeStruct((slots,) + block, BF16),
            jax.ShapeDtypeStruct(block, BF16),
            jax.ShapeDtypeStruct(block, BF16),
        ),
        in_specs=[SMEM, SMEM] + [VMEM] * 4,
        out_specs=(VMEM,) * 3,
        scratch_shapes=[pltpu.VMEM((split + 2 * mine.shape[0],) + block, BF16)],
        compiler_params=PARAMS,
        name="leaf_backward",
    )(rows, count, whole, mine, other, store)


def exchange(blocks, axes):
    return lax.all_to_all(blocks, axes, 0, 0, tiled=True)


def swapped(array):
    return lax.ppermute(array, "core", [(0, 1), (1, 0)])


def body(
    leaf_rhs,
    leaf_inverse,
    leaf_panel,
    panel_rows,
    live_count,
    sep1_rhs,
    sep1_inverse,
    sep1_panel,
    sep2_rhs,
    sep2_inverse,
):
    rhs, inverse, panels = leaf_rhs[0, 0], leaf_inverse[0, 0], leaf_panel[0, 0]
    rows = panel_rows[0, 0]
    inverse1, inverse2, panel1 = sep1_inverse[0, 0], sep2_inverse[0, 0], sep1_panel[0, 0]
    width = inverse.shape[1]
    first_blocks = inverse1.shape[0] // width
    second_blocks = inverse2.shape[0] // width
    rows1, rows2 = inverse1.shape[0], inverse2.shape[0]
    places = store_rows(rows1, rows2, rows.shape[0], rows.shape[1], width)
    panel1_at, inverse2_at = places[0]["panel1"], places[0]["inverse2"]
    terms_at = places[0]["terms"]

    send1, store, keep = leaf_forward(
        places,
        live_count,
        rows,
        rhs,
        inverse,
        panels,
        sep1_rhs[0, 0],
        sep2_rhs[0, 0],
        inverse1,
        panel1,
        inverse2,
    )
    other = swapped(store)
    partial1 = first_partials(exchange(send1, FIRST), store, rows1)
    raised, solved1_t = raise_terms(
        exchange(partial1, FIRST), keep, store, other, panel1_at, rows2, terms_at
    )
    partial2 = side_partials(exchange(raised, CHIPS), store, other, inverse2_at, rows2)
    whole_solved = exchange(turned_sum(exchange(partial2, CHIPS)), CHIPS)

    whole_second = exchange(
        back_step(whole_solved, store, other, inverse2_at, second_blocks // 2), CHIPS
    )
    shifted = back_step(whole_second, store, other, panel1_at, first_blocks // 2, solved1_t)
    whole_shifted = exchange(shifted, LINE)
    other_second = swapped(lax.optimization_barrier((whole_second, shifted))[0])
    sample1_t, other_second = lax.optimization_barrier(
        (back_step(whole_shifted, store, other, 0, first_blocks), other_second)
    )
    whole_first = exchange(sample1_t, FIRST)
    leaf_sample, sample1, sample2 = leaf_backward(
        places, rows, live_count, whole_first, whole_second, other_second, store
    )
    return (leaf_sample[None, None], sample1[None, None], sample2[None, None])


def solution(mesh):
    places = mesh.devices.reshape(-1, 2, 2, mesh.shape["panel"])
    fine = Mesh(places, ("group", "pair", "core", "panel"))
    leaf = ("group", "pair", "core")

    def spec(rank):
        return P("panel", leaf, *(None,) * (rank - 2))

    return jax.shard_map(
        body,
        mesh=fine,
        in_specs=tuple(spec(rank) for rank in (5, 5, 6, 4, 2, 4, 4, 4, 4, 4)),
        out_specs=tuple(spec(rank) for rank in (5, 4, 4)),
        check_vma=False,
    )
```

```python
import jax
import jax.numpy as jnp
from jax import lax
from jax.experimental import pallas as pl
from jax.experimental.pallas import tpu as pltpu
from jax.sharding import Mesh, PartitionSpec as P

FIRST = ("core", "panel")
CHIPS = ("pair", "panel")
LINE = ("panel",)
F32, BF16 = jnp.float32, jnp.bfloat16
VMEM = pl.BlockSpec(memory_space=pltpu.VMEM)
SMEM = pl.BlockSpec(memory_space=pltpu.SMEM)
HBM = pl.BlockSpec(memory_space=pltpu.HBM)
PARAMS = pltpu.CompilerParams(vmem_limit_bytes=24 << 20)


def in_hbm(*arrays):
    return [pltpu.with_memory_space_constraint(array, pltpu.HBM) for array in arrays]


def dot(left, right):
    return lax.dot_general(left, right, (((1,), (0,)), ((), ())), preferred_element_type=F32)


def half_lanes(block):
    return lax.broadcasted_iota(jnp.int32, block.shape, 1) < block.shape[1] // 2


def turned(block):
    return pltpu.roll(block, block.shape[1] // 2, 1)


def packed(lower, upper):
    low = half_lanes(lower)
    return jnp.where(low, lower, turned(upper)), jnp.where(low, turned(lower), upper)


def start_loads(sems, *pairs):
    loads = [pltpu.make_async_copy(*pair, sems.at[i]) for i, pair in enumerate(pairs)]
    for load in loads:
        load.start()
    return loads


def store_rows(rows1, rows2, slots, touched, width):
    sizes = {
        "inverse1": rows1,
        "panel1": rows2,
        "inverse2": rows2,
        "terms": rows2 // 2,
        "panels": slots * touched * width,
        "inverse": slots * width,
        "solved": slots * width,
    }
    places, end = {}, 0
    for name, size in sizes.items():
        places[name] = end
        end += size
    return places, end


def leaf_forward(
    places, count, rows, rhs, inverse, panels, side1, side2, inverse1, panel1, inverse2
):
    block = rhs.shape[1:]
    width = block[0]
    slots, touched = rows.shape
    first_blocks, second_blocks = inverse1.shape[0] // width, inverse2.shape[0] // width
    halves, line = second_blocks // 2, first_blocks // 2
    own_rows, all_rows = places

    def kernel(
        rows_h,
        count,
        rhs,
        inverse,
        panels,
        side1,
        side2,
        inverse1,
        panel1,
        inverse2,
        send,
        store,
        keep,
        total,
        rows,
        rhs_v,
        side1_v,
        side2_v,
        sems,
        more_sems,
    ):
        def part(name, start=0, size=None, of=None):
            first = own_rows[name] + start
            return slice(first, first + (of.shape[0] if size is None else size))

        loads = start_loads(
            sems,
            (inverse, store.at[part("inverse", of=inverse)]),
            (rhs, rhs_v),
            (panels, store.at[part("panels", of=panels)]),
            (rows_h, rows),
            (side1, side1_v),
            (side2, side2_v),
        )
        matrices = start_loads(
            more_sems,
            (inverse1, store.at[part("inverse1", of=inverse1)]),
            (panel1, store.at[part("panel1", of=panel1)]),
            (inverse2, store.at[part("inverse2", of=inverse2)]),
        )
        core = lax.axis_index("core")
        total[...] = jnp.zeros_like(total)
        loads[0].wait()
        loads[1].wait()
        solved = []
        for s in range(slots):
            live = jnp.where(s < count[0, 0], 1.0, 0.0)
            piece = dot(store[part("inverse", s * width, width)], rhs_v[s]) * live
            piece = piece.astype(BF16)
            store[part("solved", s * width, width)] = piece.astype(F32).T.astype(BF16)
            solved.append(piece)
        loads[2].wait()
        loads[3].wait()
        for s in range(slots):
            tall = touched * width
            products = dot(store[part("panels", s * tall, tall)], solved[s])
            for k in range(touched):
                total[rows[s, k]] += products[k * width : (k + 1) * width]
        loads[4].wait()
        loads[5].wait()
        own = core * line + lax.axis_index("panel")
        total[own] -= side1_v[...].astype(F32)
        own = own + (lax.axis_index("pair") + 1) * first_blocks
        total[own] -= side2_v[...].astype(F32)
        for p in range(line):
            zero, one = packed(total[p], total[line + p])
            send[p] = zero.astype(BF16)
            send[line + p] = one.astype(BF16)
        for z in range(2):
            for p in range(line):
                at = (z + 1) * first_blocks + p
                zero, one = packed(total[at], total[at + line])
                at = z * line + p
                keep[at] = jnp.where(core == 0, zero, one)
                away = jnp.where(core == 0, one, zero)
                store[part("terms", at * width, width)] = away.astype(BF16)
        for load in matrices:
            load.wait()

    arrays = in_hbm(
        rhs,
        inverse.reshape(-1, width),
        panels.reshape(-1, width),
        side1,
        side2,
        inverse1,
        panel1,
        inverse2,
    )
    return pl.pallas_call(
        kernel,
        out_shape=(
            jax.ShapeDtypeStruct((first_blocks,) + block, BF16),
            jax.ShapeDtypeStruct((all_rows, width), BF16),
            jax.ShapeDtypeStruct((halves,) + block, F32),
        ),
        in_specs=[HBM, SMEM] + [HBM] * len(arrays),
        out_specs=(VMEM,) * 3,
        scratch_shapes=[
            pltpu.VMEM((first_blocks + second_blocks,) + block, F32),
            pltpu.SMEM(rows.shape, rows.dtype),
            pltpu.VMEM(rhs.shape, BF16),
            pltpu.VMEM(side1.shape, BF16),
            pltpu.VMEM(side2.shape, BF16),
            pltpu.SemaphoreType.DMA((6,)),
            pltpu.SemaphoreType.DMA((3,)),
        ],
        compiler_params=PARAMS,
        name="leaf_forward",
    )(*in_hbm(rows), count, *arrays)


def column_products(piece, mine, other, first_row, row_count):
    low = half_lanes(piece)
    across = turned(piece)
    zero = jnp.zeros_like(piece)
    lower = (jnp.where(low, piece, zero), jnp.where(low, across, zero))
    upper = (jnp.where(low, zero, across), jnp.where(low, zero, piece))
    swap = lax.axis_index("core") == 1

    def ordered(two):
        return [jnp.where(swap, two[1], two[0]), jnp.where(swap, two[0], two[1])]

    weights = jnp.concatenate(ordered(lower) + ordered(upper), 0).astype(BF16)
    half = mine.shape[1] * 4
    parts = []
    for start in range(first_row, first_row + row_count, 2 * half):
        middle = start + half
        wide = jnp.concatenate(
            [
                mine[start:middle],
                other[start:middle],
                mine[middle : middle + half],
                other[middle : middle + half],
            ],
            1,
        )
        parts.append(dot(wide, weights))
    return parts


def side_partials(received, mine, other, first_row, row_count):
    width = mine.shape[1]

    def kernel(received, mine, other, partials):
        side = -received[...].astype(F32).sum(axis=0)
        side = side.astype(BF16).astype(F32)
        for z, part in enumerate(column_products(side, mine, other, first_row, row_count)):
            for p in range(4):
                partials[z * 4 + p] = part[p * width : (p + 1) * width].astype(BF16)

    return pl.pallas_call(
        kernel,
        out_shape=jax.ShapeDtypeStruct((row_count // width // 2,) + received.shape[1:], BF16),
        in_specs=[VMEM] * 3,
        out_specs=VMEM,
        compiler_params=PARAMS,
        name="side_partials",
    )(received, mine, other)


def raise_terms(received, keep, mine, other, first_row, row_count, terms_row):
    width = mine.shape[1]

    def kernel(received, keep, mine, other, raised, solved_t):
        piece = received[...].astype(F32).sum(axis=0)
        piece = piece.astype(BF16).astype(F32)
        for z, part in enumerate(column_products(piece, mine, other, first_row, row_count)):
            for p in range(4):
                at = z * 4 + p
                came = other[terms_row + at * width : terms_row + (at + 1) * width]
                terms = keep[at] + came.astype(F32)
                raised[at] = (part[p * width : (p + 1) * width] + terms).astype(BF16)
        solved_t[...] = piece.T.astype(BF16)

    return pl.pallas_call(
        kernel,
        out_shape=(
            jax.ShapeDtypeStruct(keep.shape, BF16),
            jax.ShapeDtypeStruct(received.shape[1:], BF16),
        ),
        in_specs=[VMEM] * 4,
        out_specs=(VMEM,) * 2,
        compiler_params=PARAMS,
        name="raise_terms",
    )(received, keep, mine, other)


def turn_kernel(received, copies):
    piece = received[...].astype(F32).sum(axis=0).T.astype(BF16)
    for i in range(copies.shape[0]):
        copies[i] = piece


def turned_sum(received):
    return pl.pallas_call(
        turn_kernel,
        out_shape=jax.ShapeDtypeStruct(received.shape, BF16),
        in_specs=[VMEM],
        out_specs=VMEM,
        compiler_params=PARAMS,
        name="turned_sum",
    )(received)


def back_step(whole, mine, other, first_row, targets, base=None):
    panels = 4
    half = whole.shape[1] // 2
    rows = pl.ds(first_row, 2 * whole.shape[0] * mine.shape[1])

    def kernel(whole, mine, other, *rest):
        pieces = []
        for z in range(whole.shape[0] // panels):
            for c in range(2):
                for p in range(panels):
                    pieces.append(whole[z * panels + p, c * half : (c + 1) * half])
        vectors = jnp.concatenate(pieces, 1)
        mine_t = dot(vectors, mine[rows])
        other_t = dot(vectors, other[rows])
        swap = lax.axis_index("core") == 1
        result = jnp.concatenate(
            [jnp.where(swap, other_t, mine_t), jnp.where(swap, mine_t, other_t)], 0
        )
        if base is not None:
            result = rest[0][...].astype(F32) - result
        copies = rest[-1]
        result = result.astype(BF16)
        for i in range(targets):
            copies[i] = result

    operands = (whole, mine, other) + (() if base is None else (base,))
    return pl.pallas_call(
        kernel,
        out_shape=jax.ShapeDtypeStruct((targets,) + whole.shape[1:], BF16),
        in_specs=[VMEM] * len(operands),
        out_specs=VMEM,
        compiler_params=PARAMS,
        name="back_step",
    )(*operands)


def leaf_backward(places, rows, count, whole, mine, other, store):
    slots, touched = rows.shape
    width = whole.shape[1]
    half = width // 2
    split = whole.shape[0]
    line = split // 2
    own_rows, _ = places

    def kernel(rows, count, whole, mine, other, store, sample, sample1, sample2, above):
        core = lax.axis_index("core")
        here = pl.ds(pl.multiple_of(core * half, half), half)
        there = pl.ds(pl.multiple_of((1 - core) * half, half), half)
        for c in range(2):
            part = slice(c * half, (c + 1) * half)
            for p in range(line):
                for h in range(2):
                    above[c * line + p, h * half : (h + 1) * half] = whole[h * line + p, part]
                for z in range(2):
                    at = (z + 1) * split + c * line + p
                    above[at, here] = mine[z * line + p, part]
                    above[at, there] = other[z * line + p, part]

        def stored(name, slot, size):
            first = own_rows[name] + slot * size
            return store[first : first + size]

        for s in range(slots):
            vectors = jnp.concatenate([above[rows[s, k]] for k in range(touched)], 1)
            correction = dot(vectors, stored("panels", s, touched * width))
            shifted = stored("solved", s, width).astype(F32) - correction
            live = jnp.where(s < count[0, 0], 1.0, 0.0)
            result = dot(shifted.astype(BF16), stored("inverse", s, width)) * live
            sample[s] = result.T.astype(BF16)
        own = core * line + lax.axis_index("panel")
        sample1[...] = above[own].astype(F32).T.astype(BF16)
        own = own + (lax.axis_index("pair") + 1) * split
        sample2[...] = above[own].astype(F32).T.astype(BF16)

    block = whole.shape[1:]
    return pl.pallas_call(
        kernel,
        out_shape=(
            jax.ShapeDtypeStruct((slots,) + block, BF16),
            jax.ShapeDtypeStruct(block, BF16),
            jax.ShapeDtypeStruct(block, BF16),
        ),
        in_specs=[SMEM, SMEM] + [VMEM] * 4,
        out_specs=(VMEM,) * 3,
        scratch_shapes=[pltpu.VMEM((split + 2 * mine.shape[0],) + block, BF16)],
        compiler_params=PARAMS,
        name="leaf_backward",
    )(rows, count, whole, mine, other, store)


def exchange(blocks, axes):
    return lax.all_to_all(blocks, axes, 0, 0, tiled=True)


def swapped(array):
    return lax.ppermute(array, "core", [(0, 1), (1, 0)])


def body(
    leaf_rhs,
    leaf_inverse,
    leaf_panel,
    panel_rows,
    live_count,
    sep1_rhs,
    sep1_inverse,
    sep1_panel,
    sep2_rhs,
    sep2_inverse,
):
    rhs, inverse, panels = leaf_rhs[0, 0], leaf_inverse[0, 0], leaf_panel[0, 0]
    rows = panel_rows[0, 0]
    inverse1, inverse2, panel1 = sep1_inverse[0, 0], sep2_inverse[0, 0], sep1_panel[0, 0]
    width = inverse.shape[1]
    first_blocks = inverse1.shape[0] // width
    second_blocks = inverse2.shape[0] // width
    rows1, rows2 = inverse1.shape[0], inverse2.shape[0]
    places = store_rows(rows1, rows2, rows.shape[0], rows.shape[1], width)
    panel1_at, inverse2_at = places[0]["panel1"], places[0]["inverse2"]
    terms_at = places[0]["terms"]

    send1, store, keep = leaf_forward(
        places,
        live_count,
        rows,
        rhs,
        inverse,
        panels,
        sep1_rhs[0, 0],
        sep2_rhs[0, 0],
        inverse1,
        panel1,
        inverse2,
    )
    other = swapped(store)
    partial1 = side_partials(exchange(send1, FIRST), store, other, 0, rows1)
    raised, solved1_t = raise_terms(
        exchange(partial1, LINE), keep, store, other, panel1_at, rows2, terms_at
    )
    partial2 = side_partials(exchange(raised, CHIPS), store, other, inverse2_at, rows2)
    whole_solved = exchange(turned_sum(exchange(partial2, CHIPS)), CHIPS)

    whole_second = exchange(
        back_step(whole_solved, store, other, inverse2_at, second_blocks // 2), CHIPS
    )
    shifted = back_step(whole_second, store, other, panel1_at, first_blocks // 2, solved1_t)
    whole_shifted = exchange(shifted, LINE)
    other_second = swapped(lax.optimization_barrier((whole_second, shifted))[0])
    whole_shifted, other_second = lax.optimization_barrier((whole_shifted, other_second))
    whole_first = exchange(back_step(whole_shifted, store, other, 0, first_blocks), FIRST)
    leaf_sample, sample1, sample2 = leaf_backward(
        places, rows, live_count, whole_first, whole_second, other_second, store
    )
    return (leaf_sample[None, None], sample1[None, None], sample2[None, None])


def solution(mesh):
    places = mesh.devices.reshape(-1, 2, 2, mesh.shape["panel"])
    fine = Mesh(places, ("group", "pair", "core", "panel"))
    leaf = ("group", "pair", "core")

    def spec(rank):
        return P("panel", leaf, *(None,) * (rank - 2))

    return jax.shard_map(
        body,
        mesh=fine,
        in_specs=tuple(spec(rank) for rank in (5, 5, 6, 4, 2, 4, 4, 4, 4, 4)),
        out_specs=tuple(spec(rank) for rank in (5, 4, 4)),
        check_vma=False,
    )
```
